32 devices in a mesh: depth: 4 (over z), height: 8 (over y, x, core).
Axes of the slice: x: 2, y: 2, z: 4, core: 2. Of those that a mesh axis runs over, the one named last changes fastest.
Arguments:
- grad_out: bfloat16 [4, 16, 64, 1024], P('depth', 'height'), may hold values from -6 to 6
- pre_act: bfloat16 [4, 16, 64, 1024], P('depth', None, None, 'height'), may hold values from -6 to 6
- w_in: bfloat16 [1024, 1024], P('depth'), may hold values from -0.1875 to 0.1875
- w_out: bfloat16 [1024, 1024], P('depth'), may hold values from -0.1875 to 0.1875
- kernel: bfloat16 [27, 32, 1024], P(None, None, 'height'), may hold values from -0.21875 to 0.21875
Outputs:
- grad_in: bfloat16 [4, 16, 64, 1024], P('depth', 'height')
- kernel_grad: float32 [27, 32, 1024], P(None, None, 'height')
The draws below stay inside these ranges and needn't reach their ends.
All inputs are finite; a program needn't handle non-finite values.
Results may differ from the reference program's by a relative error of at most 0.014.
Values may be sent and summed in bfloat16 or wider, within the bound.
No kernel may reach another device: no remote copies, remote signals or barrier semaphores. Data moves between devices by JAX's collectives and lax.ppermute only.
A program may use at most 64 MiB of HBM per device.

```python
import jax
import jax.numpy as jnp
from jax import lax

C = 1024
CG = 32
WID = 64
DT = 4
HT = 16
CELLS = 4096


def block_scale(own_key, extent, shards, smallest, top_value):
    factor_of, own = 1.0, jax.random.fold_in(own_key, 6)
    for dim, blocks in shards:
        steps = jnp.exp(jax.random.uniform(jax.random.fold_in(own, dim), (blocks,), jnp.float32, smallest / len(shards), top_value / len(shards)))
        factor_of = factor_of * jnp.repeat(steps, extent[dim] // blocks).reshape([-1 if axis == dim else 1 for axis in range(len(extent))])
    return factor_of


def normal_values(key, shape, scale, bound, split=(), dtype=jnp.bfloat16):
    result = scale * jax.random.normal(key, shape, jnp.float32)
    if split:
        result = result * block_scale(key, shape, split, -0.22, 0.18)
    return jnp.clip(result, -bound, bound).astype(dtype)


def setup_inputs(seed: int = 0) -> dict:
    splits = jax.random.split(jax.random.key(seed), 6)
    grad_out = normal_values(splits[0], (DT, HT, WID, C), 1.0, 6.0, ((0, 4), (1, 8)))
    pre_act = normal_values(splits[1], (DT, HT, WID, C), 1.0, 6.0, ((0, 4), (3, 8)))
    w_in = normal_values(splits[2], (C, C), C ** -0.5, 0.1875, ((0, 4),))
    w_out = normal_values(splits[3], (C, C), C ** -0.5, 0.1875, ((0, 4),))
    kernel = normal_values(splits[4], (27, CG, C), (27 * CG) ** -0.5, 0.21875, ((2, 8),))
    return dict(grad_out=grad_out, pre_act=pre_act, w_in=w_in, w_out=w_out, kernel=kernel)


def reference(grad_out, pre_act, w_in, w_out, kernel):
    depth_len, height_len, width_len, chans = grad_out.shape
    group_width = kernel.shape[1]
    group_count = chans // group_width
    flat = grad_out.reshape(-1, chans)
    grad_mid = jnp.dot(flat, w_out.T, preferred_element_type=jnp.float32).astype(jnp.bfloat16)
    grad_mid = grad_mid.reshape(depth_len, height_len, width_len, group_count, group_width)
    moved = jnp.moveaxis(grad_mid, 3, 0)
    pre_groups = jnp.moveaxis(pre_act.reshape(depth_len, height_len, width_len, group_count, group_width), 3, 0)
    kern = jnp.transpose(kernel.reshape(27, group_width, group_count, group_width), (2, 0, 1, 3))

    def per_group(items):
        mid, pre, weights = items
        hidden = jnp.maximum(pre, 0).astype(jnp.float32)
        padded = jnp.pad(mid.astype(jnp.float32), ((1, 1), (1, 1), (1, 1), (0, 0)))
        back = jnp.zeros(hidden.shape, jnp.float32)
        grads = []
        for step_d in (-1, 0, 1):
            for step_h in (-1, 0, 1):
                for step_w in (-1, 0, 1):
                    index = 9 * (step_d + 1) + 3 * (step_h + 1) + (step_w + 1)
                    window = padded[1 - step_d:1 - step_d + depth_len, 1 - step_h:1 - step_h + height_len, 1 - step_w:1 - step_w + width_len, :]
                    back = back + jnp.einsum('dhwo,io->dhwi', window, weights[index].astype(jnp.float32))
                    grads.append(jnp.einsum('dhwo,dhwi->io', window, hidden))
        masked = jnp.where(pre > 0, back, jnp.zeros_like(back)).astype(jnp.bfloat16)
        return masked, jnp.stack(grads)

    masked, kgrads = lax.map(per_group, (moved, pre_groups, kern))
    grad_pre = jnp.moveaxis(masked, 0, 3).reshape(depth_len, height_len, width_len, chans)
    scale = jnp.float32(CELLS) ** -0.5
    kernel_grad = jnp.transpose(kgrads, (1, 2, 0, 3)).reshape(27, group_width, chans) * scale
    branch = jnp.dot(grad_pre.reshape(-1, chans), w_in.T, preferred_element_type=jnp.float32)
    grad_in = (grad_out.astype(jnp.float32) + branch.reshape(grad_out.shape)).astype(jnp.bfloat16)
    return grad_in, kernel_grad
```

```python
import functools

import jax
import jax.numpy as jnp
from jax import lax
from jax.experimental import pallas as pl
from jax.experimental.pallas import tpu as pltpu
from jax.sharding import PartitionSpec as P

F32 = jnp.float32
BF16 = jnp.bfloat16
NT = (((1,), (1,)), ((), ()))
TN = (((0,), (0,)), ((), ()))
VMEM_LIMIT = 48 * 1024 * 1024


def vmem():
    return pl.BlockSpec(memory_space=pltpu.VMEM)


def smem():
    return pl.BlockSpec(memory_space=pltpu.SMEM)


def call(body, out_shape, n_in, *, scalars=1, scratch=(), flops=0, nbytes=0):
    return pl.pallas_call(
        body,
        out_shape=out_shape,
        in_specs=[smem()] * scalars + [vmem()] * n_in,
        out_specs=jax.tree.map(lambda _: vmem(), out_shape),
        scratch_shapes=list(scratch),
        compiler_params=pltpu.CompilerParams(vmem_limit_bytes=VMEM_LIMIT),
        cost_estimate=pl.CostEstimate(flops=flops, bytes_accessed=nbytes, transcendentals=0),
    )


def swap(x, axis, mask):
    n = lax.axis_size(axis)
    return lax.ppermute(x, axis, [(i, i ^ mask) for i in range(n)])


def shift(x, axis, step):
    n = lax.axis_size(axis)
    return lax.ppermute(x, axis, [(i, i + step) for i in range(n) if 0 <= i + step < n])


def fetch_rows(w, me_core):
    planes, cols = lax.axis_size("depth"), lax.axis_size("height")
    chips = cols // 2
    part = w.shape[0] // 2
    mine = lax.dynamic_slice_in_dim(w, me_core * part, part, axis=0)
    pairs = []
    for d in range(planes):
        for h in range(cols):
            pairs.append((d * cols + h, (d ^ (h // 2)) * cols + 2 * d + h % 2))
    del chips
    return lax.ppermute(mine, ("depth", "height"), pairs)


def plane_gather(x):
    half = x.shape[0] // 2
    across_x, across_y = swap(x, "height", 2), swap(x, "height", 4)
    core = swap(x, "height", 1)
    diag_a = swap(across_x[:half], "height", 4)
    diag_b = swap(across_y[half:], "height", 2)
    return [
        (0, 0, x),
        (1, 0, core),
        (2, 0, across_x),
        (3, 0, swap(across_x, "height", 1)),
        (4, 0, across_y),
        (5, 0, swap(across_y, "height", 1)),
        (6, 0, diag_a),
        (6, half, diag_b),
        (7, 0, swap(diag_a, "height", 1)),
        (7, half, swap(diag_b, "height", 1)),
    ]


def mid_body(places, rows, h_ref, w_ref, *refs):
    blocks, out = refs[:-1], refs[-1]
    h = h_ref[0]
    w = w_ref[...]
    for (mask, first), block in zip(places, blocks):
        n = block.shape[0]
        at = pl.multiple_of((h ^ mask) * rows + first, 16)
        out[pl.ds(at, n), :] = lax.dot_general(
            block[...], w, NT, preferred_element_type=F32
        ).astype(BF16)


def kgrad_body(wid, group, mid, own, up, down, out, pad):
    cells, chans = mid.shape
    g32 = mid[...].astype(F32)
    col = lax.broadcasted_iota(jnp.int32, (cells, 1), 0) % wid
    left = jnp.where(col < wid - 1, pltpu.roll(g32, cells - 1, 0), 0.0).astype(BF16)
    right = jnp.where(col > 0, pltpu.roll(g32, 1, 0), 0.0).astype(BF16)
    rhs = jnp.concatenate([left, mid[...], right], axis=1)
    zero = jnp.zeros((wid, chans), BF16)
    lane_group = lax.broadcasted_iota(jnp.int32, (group, chans), 1) // group
    for s, plane in enumerate((down, own, up)):
        pad[0:wid, :] = zero
        pad[wid + cells : 2 * wid + cells, :] = zero
        pad[wid : wid + cells, :] = jnp.maximum(plane[...], jnp.zeros((), BF16))
        for t in range(3):
            lhs = pad[t * wid : t * wid + cells, :]
            res = lax.dot_general(lhs, rhs, TN, preferred_element_type=F32)
            for u in range(3):
                tile = res[:, u * chans : (u + 1) * chans]
                acc = jnp.zeros((group, chans), F32)
                for g in range(chans // group):
                    acc = jnp.where(lane_group == g, tile[g * group : (g + 1) * group, :], acc)
                out[9 * s + 3 * t + u] = acc.astype(BF16)


def back_body(wid, mid, lower, upper, pre, weights, out, pad):
    cells, chans = mid.shape
    zero = jnp.zeros((wid, chans), BF16)
    for s, plane in enumerate((upper, mid, lower)):
        pad[s, 0:wid, :] = zero
        pad[s, wid + cells : 2 * wid + cells, :] = zero
        pad[s, wid : wid + cells, :] = plane[...]
    col = lax.broadcasted_iota(jnp.int32, (256, 1), 0) % wid
    for c in range(cells // 256):
        lhs = jnp.concatenate(
            [pad[s, (2 - t) * wid + 256 * c : (2 - t) * wid + 256 * c + 256, :] for s in range(3) for t in range(3)],
            axis=1,
        )
        y = lax.dot_general(lhs, weights[...], NT, preferred_element_type=F32)
        total = y[:, chans : 2 * chans]
        total = total + jnp.where(col < wid - 1, pltpu.roll(y[:, :chans], 255, 0), 0.0)
        total = total + jnp.where(col > 0, pltpu.roll(y[:, 2 * chans :], 1, 0), 0.0)
        rows = slice(256 * c, 256 * c + 256)
        out[rows, :] = jnp.where(pre[rows, :].astype(F32) > 0, total, 0.0).astype(BF16)


def final_body(grad, w, skip, out):
    lhs = jnp.concatenate([grad[i] for i in range(grad.shape[0])], axis=1)
    acc = lax.dot_general(lhs, w[...], NT, preferred_element_type=F32)
    out[...] = (skip[...].astype(F32) + acc).astype(BF16)


def block_weights(kernel, chans, group):
    groups = chans // group
    row_group = jnp.arange(chans)[:, None] // group
    lane_group = jnp.arange(chans)[None, :] // group
    tiled = jnp.tile(kernel, (1, groups, 1))
    tiled = jnp.where(row_group == lane_group, tiled, jnp.zeros_like(tiled))
    tiled = tiled.reshape(9, 3, chans, chans)
    return jnp.transpose(tiled, (1, 2, 0, 3)).reshape(3 * chans, 9 * chans)


def sum_depth(part):
    n = lax.axis_size("depth")
    mask = 1
    while mask < n:
        part = part.astype(BF16)
        part = part.astype(F32) + swap(part, "depth", mask).astype(F32)
        mask *= 2
    return part


def fast(grad_out, pre_act, w_in, w_out, kernel):
    _, rows_here, wid, width = grad_out.shape
    _, height, _, chans = pre_act.shape
    group = kernel.shape[1]
    block = rows_here * wid
    cells = height * wid
    h = lax.axis_index("height")
    h_arr = h.astype(jnp.int32).reshape(1)
    skip = grad_out.reshape(block, width)
    pre = pre_act.reshape(cells, chans)

    gathered = plane_gather(skip)
    w_rows = fetch_rows(w_out, h % 2)
    w_full = lax.all_gather(w_in, "depth", axis=0, tiled=True)
    pre_lower, pre_upper = shift(pre, "depth", 1), shift(pre, "depth", -1)
    weights = block_weights(kernel, chans, group)

    places = [(mask, first) for mask, first, _ in gathered]
    mid = call(
        functools.partial(mid_body, places, block),
        jax.ShapeDtypeStruct((cells, chans), BF16),
        1 + len(places),
        flops=2 * cells * width * chans,
        nbytes=2 * cells * width,
    )(h_arr, w_rows, *[b for _, _, b in gathered])

    lower, upper = shift(mid, "depth", 1), shift(mid, "depth", -1)
    part = call(
        functools.partial(kgrad_body, wid, group),
        jax.ShapeDtypeStruct((27, group, chans), BF16),
        4,
        scalars=0,
        scratch=[pltpu.VMEM((cells + 2 * wid, chans), BF16)],
        flops=2 * 27 * chans * chans * cells,
        nbytes=10 * cells * chans,
    )(mid, pre, pre_upper, pre_lower)
    total_cells = cells * lax.axis_size("depth")
    scale = jnp.float32(total_cells) ** (-0.5)
    kernel_grad = sum_depth(part) * scale

    back = call(
        functools.partial(back_body, wid),
        jax.ShapeDtypeStruct((cells, chans), BF16),
        5,
        scalars=0,
        scratch=[pltpu.VMEM((3, cells + 2 * wid, chans), BF16)],
        flops=2 * 27 * chans * chans * cells,
        nbytes=10 * cells * chans,
    )(mid, lower, upper, pre, weights)

    parts = lax.all_to_all(back.reshape(cells // block, block, chans), "height", 0, 0)
    grad_in = call(
        final_body,
        jax.ShapeDtypeStruct((block, width), BF16),
        3,
        scalars=0,
        flops=2 * block * width * width,
        nbytes=2 * width * width,
    )(parts, w_full, skip)
    return grad_in.reshape(grad_out.shape), kernel_grad


def with_halo(cells, axis, dim, width):
    head = lax.slice_in_dim(cells, 0, width, axis=dim)
    tail = lax.slice_in_dim(cells, cells.shape[dim] - width, cells.shape[dim], axis=dim)
    return jnp.concatenate([shift(tail, axis, 1), cells, shift(head, axis, -1)], axis=dim)


def general(grad_out, pre_act, w_in, w_out, kernel):
    product = lax.dot_general(
        grad_out,
        lax.all_gather(w_out, "depth", axis=0, tiled=True),
        (((3,), (1,)), ((), ())),
        preferred_element_type=F32,
    )
    grad_mid = product.astype(BF16)
    grouped = lax.all_to_all(grad_mid, "height", split_axis=3, concat_axis=1, tiled=True)
    padded = with_halo(grouped, "depth", 0, 1)
    padded = jnp.pad(padded, ((0, 0), (1, 1), (1, 1), (0, 0)))
    depth_len, height_len, width_len, chans = pre_act.shape
    group = kernel.shape[1]
    groups = chans // group
    hidden = jnp.maximum(pre_act, jnp.zeros_like(pre_act)).reshape(
        depth_len, height_len, width_len, groups, group
    )
    kern = kernel.reshape(27, group, groups, group)
    back = jnp.zeros((groups, group, depth_len, height_len, width_len), F32)
    grads = []
    for s in range(3):
        windows = [
            padded[2 - s : 2 - s + depth_len, 2 - t : 2 - t + height_len, 2 - u : 2 - u + width_len, :]
            for t in range(3)
            for u in range(3)
        ]
        stacked = jnp.concatenate(windows, axis=3)
        stacked = stacked.reshape(depth_len, height_len, width_len, 9, groups, group)
        back = back + jnp.einsum(
            "dhwkgj,kigj->gidhw", stacked, kern[9 * s : 9 * s + 9], preferred_element_type=F32
        )
        grads.append(jnp.einsum("dhwkgj,dhwgi->kigj", stacked, hidden, preferred_element_type=F32))
    back = jnp.transpose(back, (2, 3, 4, 0, 1)).reshape(depth_len, height_len, width_len, chans)
    grad_pre = jnp.where(pre_act > 0, back, jnp.zeros_like(back)).astype(BF16)
    part = jnp.concatenate(grads, axis=0).reshape(27, group, chans)
    total_cells = depth_len * lax.axis_size("depth") * height_len * width_len
    scale = jnp.float32(total_cells) ** (-0.5)
    kernel_grad = lax.psum(part.astype(BF16), "depth").astype(F32) * scale
    by_height = lax.all_to_all(grad_pre, "height", split_axis=1, concat_axis=3, tiled=True)
    branch = lax.dot_general(
        by_height,
        lax.all_gather(w_in, "depth", axis=0, tiled=True),
        (((3,), (1,)), ((), ())),
        preferred_element_type=F32,
    )
    return (grad_out.astype(F32) + branch).astype(BF16), kernel_grad


def solution(mesh):
    planes, cols = mesh.shape["depth"], mesh.shape["height"]

    def shards(grad_out, pre_act, w_in, w_out, kernel):
        whole_lanes = pre_act.shape[3] == 128 and pre_act.shape[0] == 1 and grad_out.shape[0] == 1
        if cols == 8 and planes == 4 and whole_lanes:
            return fast(grad_out, pre_act, w_in, w_out, kernel)
        return general(grad_out, pre_act, w_in, w_out, kernel)

    in_specs = (
        P("depth", "height", None, None),
        P("depth", None, None, "height"),
        P("depth", None),
        P("depth", None),
        P(None, None, "height"),
    )
    out_specs = (P("depth", "height", None, None), P(None, None, "height"))
    return jax.shard_map(shards, mesh=mesh, in_specs=in_specs, out_specs=out_specs, check_vma=False)
```

```python
import functools

import jax
import jax.numpy as jnp
from jax import lax
from jax.experimental import pallas as pl
from jax.experimental.pallas import tpu as pltpu
from jax.sharding import PartitionSpec as P

F32 = jnp.float32
BF16 = jnp.bfloat16
NT = (((1,), (1,)), ((), ()))
TN = (((0,), (0,)), ((), ()))
VMEM_LIMIT = 48 * 1024 * 1024


def vmem():
    return pl.BlockSpec(memory_space=pltpu.VMEM)


def smem():
    return pl.BlockSpec(memory_space=pltpu.SMEM)


def call(body, out_shape, n_in, *, scalars=1, scratch=(), flops=0, nbytes=0):
    return pl.pallas_call(
        body,
        out_shape=out_shape,
        in_specs=[smem()] * scalars + [vmem()] * n_in,
        out_specs=jax.tree.map(lambda _: vmem(), out_shape),
        scratch_shapes=list(scratch),
        compiler_params=pltpu.CompilerParams(vmem_limit_bytes=VMEM_LIMIT),
        cost_estimate=pl.CostEstimate(flops=flops, bytes_accessed=nbytes, transcendentals=0),
    )


def swap(x, axis, mask):
    n = lax.axis_size(axis)
    return lax.ppermute(x, axis, [(i, i ^ mask) for i in range(n)])


def shift(x, axis, step):
    n = lax.axis_size(axis)
    return lax.ppermute(x, axis, [(i, i + step) for i in range(n) if 0 <= i + step < n])


def order(x, *before):
    return lax.optimization_barrier((x,) + before)[0]


CARRIER = {
    (0, 1): 0, (0, 2): 1, (0, 3): 2,
    (1, 0): 1, (1, 2): 3, (1, 3): 0,
    (2, 0): 0, (2, 1): 2, (2, 3): 3,
    (3, 0): 3, (3, 1): 1, (3, 2): 2,
}


def fetch_rows(w, core):
    cols = lax.axis_size("height")
    part = w.shape[0] // 2
    mine = lax.dynamic_slice_in_dim(w, core * part, part, axis=0)
    pairs = [
        (src * cols + 2 * chip + c, dst * cols + 2 * src + c)
        for (src, dst), chip in CARRIER.items()
        for c in range(2)
    ]
    return mine, lax.ppermute(mine, ("depth", "height"), pairs)


def fetch_columns(w, core):
    planes, cols = lax.axis_size("depth"), lax.axis_size("height")
    rows, width = w.shape
    lanes = width // cols
    split = w.reshape(rows, cols // 2, 2, lanes)
    piece = lax.dynamic_index_in_dim(split, core, 2, keepdims=False).reshape(rows, width // 2)
    pairs = [(d * cols + h, (d ^ (h // 2)) * cols + h) for d in range(planes) for h in range(cols)]
    return lax.ppermute(piece, ("depth", "height"), pairs)


def chip_gather(x):
    half = x.shape[0] // 2
    across_x, across_y = swap(x, "height", 2), swap(x, "height", 4)
    diag_a = swap(across_x[:half], "height", 4)
    diag_b = swap(across_y[half:], "height", 2)
    return [(0, 0, x), (1, 0, across_x), (2, 0, across_y), (3, 0, diag_a), (3, half, diag_b)]


def plane_gather(x):
    blocks = []
    for mask, first, block in chip_gather(x):
        blocks.append((2 * mask, first, block))
        blocks.append((2 * mask + 1, first, swap(block, "height", 1)))
    return blocks


def mid_body(places, rows, here, local, fetched, *refs):
    blocks, out = refs[:-1], refs[-1]
    d, h = here[0], here[1]
    w = jnp.where(d == h // 2, local[...], fetched[...])
    for (mask, first), block in zip(places, blocks):
        n = block.shape[0]
        at = pl.multiple_of((h ^ mask) * rows + first, 16)
        out[pl.ds(at, n), :] = lax.dot_general(
            block[...], w, NT, preferred_element_type=F32
        ).astype(BF16)


def kgrad_body(wid, group, here, mid, own, near, far, out, pad):
    cells, chans = mid.shape
    g32 = mid[...].astype(F32)
    col = lax.broadcasted_iota(jnp.int32, (cells, 1), 0) % wid
    left = jnp.where(col < wid - 1, pltpu.roll(g32, cells - 1, 0), 0.0).astype(BF16)
    right = jnp.where(col > 0, pltpu.roll(g32, 1, 0), 0.0).astype(BF16)
    rhs = jnp.concatenate([left, mid[...], right], axis=1)
    zero = jnp.zeros((wid, chans), BF16)
    lane_group = lax.broadcasted_iota(jnp.int32, (group, chans), 1) // group
    odd = here[0] % 2 == 1
    below, above = jnp.where(odd, near[...], far[...]), jnp.where(odd, far[...], near[...])
    pad[0:wid, :] = zero
    pad[wid + cells : 2 * wid + cells, :] = zero
    for s, plane in enumerate((below, own[...], above)):
        pad[wid : wid + cells, :] = jnp.maximum(plane, jnp.zeros((), BF16))
        for t in range(3):
            lhs = pad[t * wid : t * wid + cells, :]
            res = lax.dot_general(lhs, rhs, TN, preferred_element_type=F32)
            for u in range(3):
                tile = res[:, u * chans : (u + 1) * chans]
                acc = jnp.zeros((group, chans), F32)
                for g in range(chans // group):
                    acc = jnp.where(lane_group == g, tile[g * group : (g + 1) * group, :], acc)
                out[9 * s + 3 * t + u] = acc.astype(BF16)


def back_body(wid, here, mid, near, far, pre, weights, *refs):
    outs, pad = refs[:-1], refs[-1]
    d, h = here[0], here[1]
    cells, chans = mid.shape
    rows = cells // len(outs)
    zero = jnp.zeros((wid, chans), BF16)
    odd = d % 2 == 1
    pad[1, wid : wid + cells, :] = mid[...]
    pad[2, wid : wid + cells, :] = jnp.where(odd, near[...], far[...])
    pad[0, wid : wid + cells, :] = jnp.where(odd, far[...], near[...])
    for s in range(3):
        pad[s, 0:wid, :] = zero
        pad[s, wid + cells : 2 * wid + cells, :] = zero
    col = lax.broadcasted_iota(jnp.int32, (rows, 1), 0) % wid
    for m, out in enumerate(outs):
        first = pl.multiple_of(((h // 2) ^ m) * rows, wid)
        lhs = jnp.concatenate(
            [pad[s, pl.ds(first + (2 - t) * wid, rows), :] for s in range(3) for t in range(3)], axis=1
        )
        y = lax.dot_general(lhs, weights[...], NT, preferred_element_type=F32)
        total = y[:, chans : 2 * chans]
        total = total + jnp.where(col < wid - 1, pltpu.roll(y[:, :chans], rows - 1, 0), 0.0)
        total = total + jnp.where(col > 0, pltpu.roll(y[:, 2 * chans :], 1, 0), 0.0)
        keep = pre[pl.ds(first, rows), :].astype(F32) > 0
        out[...] = jnp.where(keep, total, 0.0).astype(BF16)


def partial_body(places, here, skip, *refs):
    chips = 4
    grads, ws, (own, other, lhs_ref) = refs[:chips], refs[chips:-3], refs[-3:]
    d, h = here[0], here[1]
    chip, core = h // 2, h % 2
    rows = skip.shape[0]
    for m, grad in enumerate(grads):
        lhs_ref[chip ^ m] = grad[...]
    lhs = jnp.concatenate([lhs_ref[i] for i in range(chips)], axis=1)
    width = skip.shape[1] // chips
    for (mask, first), w in zip(places, ws):
        n = w.shape[0]
        acc = lax.dot_general(lhs, w[...], NT, preferred_element_type=F32)
        at = pl.ds(pl.multiple_of((d ^ chip ^ mask) * width + first, 128), n)
        here_part = jnp.where(core == 0, acc[:rows], acc[rows:])
        there_part = jnp.where(core == 0, acc[rows:], acc[:rows])
        own[:, at] = here_part + skip[:, at].astype(F32)
        other[:, at] = there_part.astype(BF16)


def block_weights(kernel, chans, group):
    groups = chans // group
    row_group = jnp.arange(chans)[:, None] // group
    lane_group = jnp.arange(chans)[None, :] // group
    tiled = jnp.tile(kernel, (1, groups, 1))
    tiled = jnp.where(row_group == lane_group, tiled, jnp.zeros_like(tiled))
    tiled = tiled.reshape(9, 3, chans, chans)
    return jnp.transpose(tiled, (1, 2, 0, 3)).reshape(3 * chans, 9 * chans)


def sum_depth(part):
    n = lax.axis_size("depth")
    mask = 1
    while mask < n:
        part = part.astype(BF16)
        part = part.astype(F32) + swap(part, "depth", mask).astype(F32)
        mask *= 2
    return part


def z_swaps(x):
    n = lax.axis_size("depth")
    between = [(i, i + 1) for i in range(1, n - 1, 2)]
    far = lax.ppermute(x, "depth", between + [(j, i) for i, j in between])
    return swap(x, "depth", 1), far


def fast(grad_out, pre_act, w_in, w_out, kernel):
    _, rows_here, wid, width = grad_out.shape
    _, height, _, chans = pre_act.shape
    group = kernel.shape[1]
    block = rows_here * wid
    cells = height * wid
    d, h = lax.axis_index("depth"), lax.axis_index("height")
    here = jnp.stack([d, h]).astype(jnp.int32)
    skip = grad_out.reshape(block, width)
    pre = pre_act.reshape(cells, chans)

    gathered = plane_gather(skip)
    local_rows, w_rows = fetch_rows(w_out, h % 2)
    pre_near, pre_far = z_swaps(pre)
    w_cols = fetch_columns(w_in, h % 2)
    weights = block_weights(kernel, chans, group)

    places = [(mask, first) for mask, first, _ in gathered]
    mid = call(
        functools.partial(mid_body, places, block),
        jax.ShapeDtypeStruct((cells, chans), BF16),
        2 + len(places),
        flops=2 * cells * width * chans,
        nbytes=2 * cells * width,
    )(here, local_rows, w_rows, *[b for _, _, b in gathered])

    near, far = z_swaps(mid)
    part = call(
        functools.partial(kgrad_body, wid, group),
        jax.ShapeDtypeStruct((27, group, chans), BF16),
        4,
        scratch=[pltpu.VMEM((cells + 2 * wid, chans), BF16)],
        flops=2 * 27 * chans * chans * cells,
        nbytes=10 * cells * chans,
    )(here, mid, pre, pre_near, pre_far)
    total_cells = cells * lax.axis_size("depth")
    scale = jnp.float32(total_cells) ** (-0.5)
    kernel_grad = sum_depth(part) * scale

    w_blocks = chip_gather(w_cols)
    chip_cells = 2 * block
    back = call(
        functools.partial(back_body, wid),
        [jax.ShapeDtypeStruct((chip_cells, chans), BF16)] * (cells // chip_cells),
        5,
        scratch=[pltpu.VMEM((3, cells + 2 * wid, chans), BF16)],
        flops=2 * 27 * chans * chans * cells,
        nbytes=10 * cells * chans,
    )(here, mid, near, far, pre, weights)
    parts = [back[0]] + [swap(b, "height", 2 * m) for m, b in enumerate(back) if m]

    own, other = call(
        functools.partial(partial_body, [(mask, first) for mask, first, _ in w_blocks]),
        [jax.ShapeDtypeStruct((block, width), F32), jax.ShapeDtypeStruct((block, width), BF16)],
        1 + len(parts) + len(w_blocks),
        scratch=[pltpu.VMEM((len(parts), chip_cells, chans), BF16)],
        flops=2 * block * width * width,
        nbytes=width * width,
    )(here, skip, *parts, *[b for _, _, b in w_blocks])
    grad_in = (own + swap(other, "height", 1).astype(F32)).astype(BF16)
    return grad_in.reshape(grad_out.shape), kernel_grad


def with_halo(cells, axis, dim, width):
    head = lax.slice_in_dim(cells, 0, width, axis=dim)
    tail = lax.slice_in_dim(cells, cells.shape[dim] - width, cells.shape[dim], axis=dim)
    return jnp.concatenate([shift(tail, axis, 1), cells, shift(head, axis, -1)], axis=dim)


def general(grad_out, pre_act, w_in, w_out, kernel):
    product = lax.dot_general(
        grad_out,
        lax.all_gather(w_out, "depth", axis=0, tiled=True),
        (((3,), (1,)), ((), ())),
        preferred_element_type=F32,
    )
    grad_mid = product.astype(BF16)
    grouped = lax.all_to_all(grad_mid, "height", split_axis=3, concat_axis=1, tiled=True)
    padded = with_halo(grouped, "depth", 0, 1)
    padded = jnp.pad(padded, ((0, 0), (1, 1), (1, 1), (0, 0)))
    depth_len, height_len, width_len, chans = pre_act.shape
    group = kernel.shape[1]
    groups = chans // group
    hidden = jnp.maximum(pre_act, jnp.zeros_like(pre_act)).reshape(
        depth_len, height_len, width_len, groups, group
    )
    kern = kernel.reshape(27, group, groups, group)
    back = jnp.zeros((groups, group, depth_len, height_len, width_len), F32)
    grads = []
    for s in range(3):
        windows = [
            padded[2 - s : 2 - s + depth_len, 2 - t : 2 - t + height_len, 2 - u : 2 - u + width_len, :]
            for t in range(3)
            for u in range(3)
        ]
        stacked = jnp.concatenate(windows, axis=3)
        stacked = stacked.reshape(depth_len, height_len, width_len, 9, groups, group)
        back = back + jnp.einsum(
            "dhwkgj,kigj->gidhw", stacked, kern[9 * s : 9 * s + 9], preferred_element_type=F32
        )
        grads.append(jnp.einsum("dhwkgj,dhwgi->kigj", stacked, hidden, preferred_element_type=F32))
    back = jnp.transpose(back, (2, 3, 4, 0, 1)).reshape(depth_len, height_len, width_len, chans)
    grad_pre = jnp.where(pre_act > 0, back, jnp.zeros_like(back)).astype(BF16)
    part = jnp.concatenate(grads, axis=0).reshape(27, group, chans)
    total_cells = depth_len * lax.axis_size("depth") * height_len * width_len
    scale = jnp.float32(total_cells) ** (-0.5)
    kernel_grad = lax.psum(part.astype(BF16), "depth").astype(F32) * scale
    by_height = lax.all_to_all(grad_pre, "height", split_axis=1, concat_axis=3, tiled=True)
    branch = lax.dot_general(
        by_height,
        lax.all_gather(w_in, "depth", axis=0, tiled=True),
        (((3,), (1,)), ((), ())),
        preferred_element_type=F32,
    )
    return (grad_out.astype(F32) + branch).astype(BF16), kernel_grad


def solution(mesh):
    planes, cols = mesh.shape["depth"], mesh.shape["height"]

    def shards(grad_out, pre_act, w_in, w_out, kernel):
        whole_lanes = pre_act.shape[3] == 128 and pre_act.shape[0] == 1 and grad_out.shape[0] == 1
        if cols == 8 and planes == 4 and whole_lanes:
            return fast(grad_out, pre_act, w_in, w_out, kernel)
        return general(grad_out, pre_act, w_in, w_out, kernel)

    in_specs = (
        P("depth", "height", None, None),
        P("depth", None, None, "height"),
        P("depth", None),
        P("depth", None),
        P(None, None, "height"),
    )
    out_specs = (P("depth", "height", None, None), P(None, None, "height"))
    return jax.shard_map(shards, mesh=mesh, in_specs=in_specs, out_specs=out_specs, check_vma=False)
```

```python
import functools

import jax
import jax.numpy as jnp
from jax import lax
from jax.experimental import pallas as pl
from jax.experimental.pallas import tpu as pltpu
from jax.sharding import PartitionSpec as P

F32 = jnp.float32
BF16 = jnp.bfloat16
NT = (((1,), (1,)), ((), ()))
TN = (((0,), (0,)), ((), ()))
VMEM_LIMIT = 48 * 1024 * 1024
SPAN = 1 << 35


def vmem():
    return pl.BlockSpec(memory_space=pltpu.VMEM)


def smem():
    return pl.BlockSpec(memory_space=pltpu.SMEM)


def call(body, out_shape, n_in, *, scalars=1, scratch=(), flops=0, nbytes=0):
    return pl.pallas_call(
        body,
        out_shape=out_shape,
        in_specs=[smem()] * scalars + [vmem()] * n_in,
        out_specs=jax.tree.map(lambda _: vmem(), out_shape),
        scratch_shapes=list(scratch),
        compiler_params=pltpu.CompilerParams(vmem_limit_bytes=VMEM_LIMIT),
        cost_estimate=pl.CostEstimate(flops=flops, bytes_accessed=nbytes, transcendentals=0),
    )


def swap(x, axis, mask):
    n = lax.axis_size(axis)
    return lax.ppermute(x, axis, [(i, i ^ mask) for i in range(n)])


def shift(x, axis, step):
    n = lax.axis_size(axis)
    return lax.ppermute(x, axis, [(i, i + step) for i in range(n) if 0 <= i + step < n])


def order(x, *before):
    return lax.optimization_barrier((x,) + before)[0]


CARRIERS = (
    {
        (0, 1): 0, (0, 2): 1, (0, 3): 2,
        (1, 0): 1, (1, 2): 3, (1, 3): 0,
        (2, 0): 0, (2, 1): 2, (2, 3): 3,
        (3, 0): 3, (3, 1): 1, (3, 2): 2,
    },
    {
        (0, 1): 1, (0, 2): 2, (0, 3): 0,
        (1, 0): 0, (1, 2): 1, (1, 3): 3,
        (2, 0): 3, (2, 1): 0, (2, 3): 2,
        (3, 0): 1, (3, 1): 2, (3, 2): 3,
    },
)


def pack_body(here, w_out, w_in, out):
    core = here[1] % 2
    part, width = w_out.shape[0] // 2, w_out.shape[1]
    out[0] = w_out[pl.ds(pl.multiple_of(core * part, part), part), :]
    lanes = width // 8
    for i in range(4):
        even = w_in[:, 2 * i * lanes : (2 * i + 1) * lanes]
        odd = w_in[:, (2 * i + 1) * lanes : (2 * i + 2) * lanes]
        block = jnp.where(core == 0, even, odd)
        for half in range(2):
            first = half * width // 2 + i * lanes
            out[1, :, first : first + lanes] = block[half * part : (half + 1) * part]


def fetch(mine):
    cols = lax.axis_size("height")
    pairs = [
        (src * cols + 2 * chip + c, dst * cols + 2 * src + c)
        for c, carrier in enumerate(CARRIERS)
        for (src, dst), chip in carrier.items()
    ]
    return lax.ppermute(mine, ("depth", "height"), pairs)


def chip_gather(x):
    half = x.shape[0] // 2
    across_x, across_y = swap(x, "height", 2), swap(x, "height", 4)
    diag_a = swap(across_x[:half], "height", 4)
    diag_b = swap(across_y[half:], "height", 2)
    return [(0, 0, x), (1, 0, across_x), (2, 0, across_y), (3, 0, diag_a), (3, half, diag_b)]


def plane_gather(chip_blocks):
    blocks = []
    for mask, first, block in chip_blocks:
        blocks.append((2 * mask, first, block))
        blocks.append((2 * mask + 1, first, swap(block, "height", 1)))
    return blocks


def mid_body(places, rows, here, local, fetched, *refs):
    blocks, (out, w_in) = refs[:-2], refs[-2:]
    d, h = here[0], here[1]
    own = d == h // 2
    w = jnp.where(own, local[0], fetched[0])
    for (mask, first), block in zip(places, blocks):
        n = block.shape[0]
        at = pl.multiple_of((h ^ mask) * rows + first, 16)
        out[pl.ds(at, n), :] = lax.dot_general(
            block[...], w, NT, preferred_element_type=F32
        ).astype(BF16)
    w_in[...] = jnp.where(own, local[1], fetched[1])


def kgrad_body(wid, group, planes, *refs):
    mids, (pre, out, pad) = refs[:planes], refs[planes:]
    cells, chans = pre.shape
    col = lax.broadcasted_iota(jnp.int32, (cells, 1), 0) % wid
    rhs = []
    for mid in mids:
        p32 = mid[...].astype(F32)
        left = jnp.where(col < wid - 1, pltpu.roll(p32, cells - 1, 0), 0.0).astype(BF16)
        right = jnp.where(col > 0, pltpu.roll(p32, 1, 0), 0.0).astype(BF16)
        rhs += [left, mid[...], right]
    rhs = jnp.concatenate(rhs, axis=1)
    lane_group = lax.broadcasted_iota(jnp.int32, (group, chans), 1) // group
    zero = jnp.zeros((wid, chans), BF16)
    pad[0:wid, :] = zero
    pad[wid + cells : 2 * wid + cells, :] = zero
    pad[wid : wid + cells, :] = jnp.maximum(pre[...], jnp.zeros((), BF16))
    for t in range(3):
        lhs = pad[t * wid : t * wid + cells, :]
        res = lax.dot_general(lhs, rhs, TN, preferred_element_type=F32)
        for p in range(planes):
            for u in range(3):
                first = (3 * p + u) * chans
                tile = res[:, first : first + chans]
                acc = jnp.zeros((group, chans), F32)
                for g in range(chans // group):
                    acc = jnp.where(lane_group == g, tile[g * group : (g + 1) * group, :], acc)
                out[p, 3 * t + u] = acc.astype(BF16)


def pair_body(here, early, late, other_early, other_late, out):
    odd = here[0] % 2
    out[1] = (early[0].astype(F32) + other_early[0].astype(F32)).astype(BF16)
    out[2 * odd] = (early[1].astype(F32) + other_late[0].astype(F32)).astype(BF16)
    out[2 - 2 * odd] = (late[0].astype(F32) + other_early[1].astype(F32)).astype(BF16)


def total_body(scale, own, other, out):
    for s in range(3):
        out[9 * s : 9 * s + 9] = (own[s].astype(F32) + other[s].astype(F32)) * scale


def back_body(wid, here, mid, near, far, pre, weights, *refs):
    outs, pad = refs[:-1], refs[-1]
    d, h = here[0], here[1]
    cells, chans = mid.shape
    rows = cells // len(outs)
    zero = jnp.zeros((wid, chans), BF16)
    odd = d % 2 == 1
    pad[1, wid : wid + cells, :] = mid[...]
    pad[2, wid : wid + cells, :] = jnp.where(odd, near[...], far[...])
    pad[0, wid : wid + cells, :] = jnp.where(odd, far[...], near[...])
    for s in range(3):
        pad[s, 0:wid, :] = zero
        pad[s, wid + cells : 2 * wid + cells, :] = zero
    col = lax.broadcasted_iota(jnp.int32, (rows, 1), 0) % wid
    for m, out in enumerate(outs):
        first = pl.multiple_of(((h // 2) ^ m) * rows, wid)
        lhs = jnp.concatenate(
            [pad[s, pl.ds(first + (2 - t) * wid, rows), :] for s in range(3) for t in range(3)], axis=1
        )
        y = lax.dot_general(lhs, weights[...], NT, preferred_element_type=F32)
        total = y[:, chans : 2 * chans]
        total = total + jnp.where(col < wid - 1, pltpu.roll(y[:, :chans], rows - 1, 0), 0.0)
        total = total + jnp.where(col > 0, pltpu.roll(y[:, 2 * chans :], 1, 0), 0.0)
        keep = pre[pl.ds(first, rows), :].astype(F32) > 0
        out[...] = jnp.where(keep, total, 0.0).astype(BF16)


def partial_body(here, skip, *refs):
    chips = 4
    grads, ws, (own, other, lhs_ref) = refs[:chips], refs[chips:-3], refs[-3:]
    chip, core = here[1] // 2, here[1] % 2
    rows = skip.shape[0]
    for m, grad in enumerate(grads):
        lhs_ref[chip ^ m] = grad[...]
    lhs = jnp.concatenate([lhs_ref[i] for i in range(chips)], axis=1)
    part, depth = ws[0].shape[0], lhs.shape[1]
    for m, w in enumerate(ws):
        for half in range(2):
            acc = lax.dot_general(
                lhs, w[:, half * depth : (half + 1) * depth], NT, preferred_element_type=F32
            )
            at = pl.ds(pl.multiple_of((chip ^ m) * 2 * part + half * part, part), part)
            here_part = jnp.where(core == 0, acc[:rows], acc[rows:])
            there_part = jnp.where(core == 0, acc[rows:], acc[:rows])
            own[:, at] = here_part + skip[:, at].astype(F32)
            other[:, at] = there_part.astype(BF16)


def weights_body(group, kernel, out):
    chans = kernel.shape[2]
    row_group = lax.broadcasted_iota(jnp.int32, (chans, chans), 0) // group
    lane_group = lax.broadcasted_iota(jnp.int32, (chans, chans), 1) // group
    zero = jnp.zeros((chans, chans), BF16)
    for o in range(27):
        st, u = o // 3, o % 3
        tiled = jnp.concatenate([kernel[o]] * (chans // group), axis=0)
        out[u * chans : (u + 1) * chans, st * chans : (st + 1) * chans] = jnp.where(
            row_group == lane_group, tiled, zero
        )


def z_swaps(x):
    n = lax.axis_size("depth")
    between = [(i, i + 1) for i in range(1, n - 1, 2)]
    far = lax.ppermute(x, "depth", between + [(j, i) for i, j in between])
    near = swap(x, "depth", 1)
    return near, far


def fast(grad_out, pre_act, w_in, w_out, kernel):
    _, rows_here, wid, width = grad_out.shape
    _, height, _, chans = pre_act.shape
    group = kernel.shape[1]
    block = rows_here * wid
    cells = height * wid
    d, h = lax.axis_index("depth"), lax.axis_index("height")
    here = jnp.stack([d, h]).astype(jnp.int32)
    skip = grad_out.reshape(block, width)
    pre = pre_act.reshape(cells, chans)

    blocks = chip_gather(skip)
    gathered = plane_gather(blocks)
    mine = call(
        pack_body, jax.ShapeDtypeStruct((2, w_out.shape[0] // 2, width), BF16), 2, nbytes=6 * w_out.size
    )(here, w_out, w_in)
    fetched = fetch(mine)
    weights = call(
        functools.partial(weights_body, group),
        jax.ShapeDtypeStruct((3 * chans, 9 * chans), BF16),
        1,
        scalars=0,
        nbytes=54 * chans * chans,
    )(order(kernel, fetched))

    places = [(mask, first) for mask, first, _ in gathered]
    mid, w_cols = call(
        functools.partial(mid_body, places, block),
        [jax.ShapeDtypeStruct((cells, chans), BF16), jax.ShapeDtypeStruct(mine.shape[1:], BF16)],
        2 + len(places),
        flops=2 * cells * width * chans,
        nbytes=2 * cells * width,
    )(here, mine, fetched, *[b for _, _, b in gathered])

    near, far = z_swaps(mid)
    kernel_flops = 2 * 9 * chans * chans * cells
    early, late = (
        call(
            functools.partial(kgrad_body, wid, group, len(planes)),
            jax.ShapeDtypeStruct((len(planes), 9, group, chans), BF16),
            len(planes) + 1,
            scalars=0,
            scratch=[pltpu.VMEM((cells + 2 * wid, chans), BF16)],
            flops=kernel_flops * len(planes),
            nbytes=6 * cells * chans,
        )(*planes, pre)
        for planes in ((mid, near), (far,))
    )
    pair = call(
        pair_body,
        jax.ShapeDtypeStruct((3, 9, group, chans), BF16),
        4,
        nbytes=100 * 9 * group * chans,
    )(here, early, late, swap(early, "depth", 1), swap(late, "depth", 1))
    total_cells = cells * lax.axis_size("depth")
    kernel_grad = call(
        functools.partial(total_body, float(total_cells) ** -0.5),
        jax.ShapeDtypeStruct((27, group, chans), F32),
        2,
        scalars=0,
        flops=SPAN,
        nbytes=24 * 9 * group * chans,
    )(pair, swap(pair, "depth", 2))

    w_blocks = [w_cols] + [swap(w_cols, "height", 2 * m) for m in (1, 2, 3)]
    chip_cells = 2 * block
    back = call(
        functools.partial(back_body, wid),
        [jax.ShapeDtypeStruct((chip_cells, chans), BF16)] * (cells // chip_cells),
        5,
        scratch=[pltpu.VMEM((3, cells + 2 * wid, chans), BF16)],
        flops=2 * 27 * chans * chans * cells,
        nbytes=10 * cells * chans,
    )(here, mid, near, far, pre, order(weights, early, late))
    parts = [back[0]] + [swap(b, "height", 2 * m) for m, b in enumerate(back) if m]

    own, other = call(
        partial_body,
        [jax.ShapeDtypeStruct((block, width), F32), jax.ShapeDtypeStruct((block, width), BF16)],
        1 + len(parts) + len(w_blocks),
        scratch=[pltpu.VMEM((len(parts), chip_cells, chans), BF16)],
        flops=SPAN,
        nbytes=width * width,
    )(here, order(skip, pair), *parts, *w_blocks)
    theirs = order(swap(other, "height", 1), kernel_grad)
    grad_in = (own + theirs.astype(F32)).astype(BF16)
    return grad_in.reshape(grad_out.shape), kernel_grad


def with_halo(cells, axis, dim, width):
    head = lax.slice_in_dim(cells, 0, width, axis=dim)
    tail = lax.slice_in_dim(cells, cells.shape[dim] - width, cells.shape[dim], axis=dim)
    return jnp.concatenate([shift(tail, axis, 1), cells, shift(head, axis, -1)], axis=dim)


def general(grad_out, pre_act, w_in, w_out, kernel):
    product = lax.dot_general(
        grad_out,
        lax.all_gather(w_out, "depth", axis=0, tiled=True),
        (((3,), (1,)), ((), ())),
        preferred_element_type=F32,
    )
    grad_mid = product.astype(BF16)
    grouped = lax.all_to_all(grad_mid, "height", split_axis=3, concat_axis=1, tiled=True)
    padded = with_halo(grouped, "depth", 0, 1)
    padded = jnp.pad(padded, ((0, 0), (1, 1), (1, 1), (0, 0)))
    depth_len, height_len, width_len, chans = pre_act.shape
    group = kernel.shape[1]
    groups = chans // group
    hidden = jnp.maximum(pre_act, jnp.zeros_like(pre_act)).reshape(
        depth_len, height_len, width_len, groups, group
    )
    kern = kernel.reshape(27, group, groups, group)
    back = jnp.zeros((groups, group, depth_len, height_len, width_len), F32)
    grads = []
    for s in range(3):
        windows = [
            padded[2 - s : 2 - s + depth_len, 2 - t : 2 - t + height_len, 2 - u : 2 - u + width_len, :]
            for t in range(3)
            for u in range(3)
        ]
        stacked = jnp.concatenate(windows, axis=3)
        stacked = stacked.reshape(depth_len, height_len, width_len, 9, groups, group)
        back = back + jnp.einsum(
            "dhwkgj,kigj->gidhw", stacked, kern[9 * s : 9 * s + 9], preferred_element_type=F32
        )
        grads.append(jnp.einsum("dhwkgj,dhwgi->kigj", stacked, hidden, preferred_element_type=F32))
    back = jnp.transpose(back, (2, 3, 4, 0, 1)).reshape(depth_len, height_len, width_len, chans)
    grad_pre = jnp.where(pre_act > 0, back, jnp.zeros_like(back)).astype(BF16)
    part = jnp.concatenate(grads, axis=0).reshape(27, group, chans)
    total_cells = depth_len * lax.axis_size("depth") * height_len * width_len
    scale = jnp.float32(total_cells) ** (-0.5)
    kernel_grad = lax.psum(part.astype(BF16), "depth").astype(F32) * scale
    by_height = lax.all_to_all(grad_pre, "height", split_axis=1, concat_axis=3, tiled=True)
    branch = lax.dot_general(
        by_height,
        lax.all_gather(w_in, "depth", axis=0, tiled=True),
        (((3,), (1,)), ((), ())),
        preferred_element_type=F32,
    )
    return (grad_out.astype(F32) + branch).astype(BF16), kernel_grad


def solution(mesh):
    planes, cols = mesh.shape["depth"], mesh.shape["height"]

    def shards(grad_out, pre_act, w_in, w_out, kernel):
        whole_lanes = pre_act.shape[3] == 128 and pre_act.shape[0] == 1 and grad_out.shape[0] == 1
        if cols == 8 and planes == 4 and whole_lanes:
            return fast(grad_out, pre_act, w_in, w_out, kernel)
        return general(grad_out, pre_act, w_in, w_out, kernel)

    in_specs = (
        P("depth", "height", None, None),
        P("depth", None, None, "height"),
        P("depth", None),
        P("depth", None),
        P(None, None, "height"),
    )
    out_specs = (P("depth", "height", None, None), P(None, None, "height"))
    return jax.shard_map(shards, mesh=mesh, in_specs=in_specs, out_specs=out_specs, check_vma=False)
```

```python
import functools

import jax
import jax.numpy as jnp
from jax import lax
from jax.experimental import pallas as pl
from jax.experimental.pallas import tpu as pltpu
from jax.sharding import PartitionSpec as P

F32 = jnp.float32
BF16 = jnp.bfloat16
NT = (((1,), (1,)), ((), ()))
TN = (((0,), (0,)), ((), ()))
VMEM_LIMIT = 48 * 1024 * 1024
SPAN = 1 << 35


def vmem():
    return pl.BlockSpec(memory_space=pltpu.VMEM)


def smem():
    return pl.BlockSpec(memory_space=pltpu.SMEM)


def call(body, out_shape, n_in, *, scalars=1, scratch=(), flops=0, nbytes=0):
    return pl.pallas_call(
        body,
        out_shape=out_shape,
        in_specs=[smem()] * scalars + [vmem()] * n_in,
        out_specs=jax.tree.map(lambda _: vmem(), out_shape),
        scratch_shapes=list(scratch),
        compiler_params=pltpu.CompilerParams(vmem_limit_bytes=VMEM_LIMIT),
        cost_estimate=pl.CostEstimate(flops=flops, bytes_accessed=nbytes, transcendentals=0),
    )


def swap(x, axis, mask):
    n = lax.axis_size(axis)
    return lax.ppermute(x, axis, [(i, i ^ mask) for i in range(n)])


def shift(x, axis, step):
    n = lax.axis_size(axis)
    return lax.ppermute(x, axis, [(i, i + step) for i in range(n) if 0 <= i + step < n])


def order(x, *before):
    return lax.optimization_barrier((x,) + before)[0]


CARRIERS = (
    {
        (0, 1): 0, (0, 2): 1, (0, 3): 2,
        (1, 0): 1, (1, 2): 3, (1, 3): 0,
        (2, 0): 0, (2, 1): 2, (2, 3): 3,
        (3, 0): 3, (3, 1): 1, (3, 2): 2,
    },
    {
        (0, 1): 1, (0, 2): 2, (0, 3): 0,
        (1, 0): 0, (1, 2): 1, (1, 3): 3,
        (2, 0): 3, (2, 1): 0, (2, 3): 2,
        (3, 0): 1, (3, 1): 2, (3, 2): 3,
    },
)


def pack_body(here, w_out, w_in, out):
    core = here[1] % 2
    part, width = w_out.shape[0] // 2, w_out.shape[1]
    out[0] = w_out[pl.ds(pl.multiple_of(core * part, part), part), :]
    lanes = width // 8
    for i in range(4):
        even = w_in[:, 2 * i * lanes : (2 * i + 1) * lanes]
        odd = w_in[:, (2 * i + 1) * lanes : (2 * i + 2) * lanes]
        block = jnp.where(core == 0, even, odd)
        for half in range(2):
            first = half * width // 2 + i * lanes
            out[1, :, first : first + lanes] = block[half * part : (half + 1) * part]


def fetch(mine):
    cols = lax.axis_size("height")
    pairs = [
        (src * cols + 2 * chip + c, dst * cols + 2 * src + c)
        for c, carrier in enumerate(CARRIERS)
        for (src, dst), chip in carrier.items()
    ]
    return lax.ppermute(mine, ("depth", "height"), pairs)


def chip_gather(x):
    half = x.shape[0] // 2
    across_x, across_y = swap(x, "height", 2), swap(x, "height", 4)
    diag_a = swap(across_x[:half], "height", 4)
    diag_b = swap(across_y[half:], "height", 2)
    return [(0, 0, x), (1, 0, across_x), (2, 0, across_y), (3, 0, diag_a), (3, half, diag_b)]


def plane_gather(chip_blocks):
    blocks = []
    for mask, first, block in chip_blocks:
        blocks.append((2 * mask, first, block))
        blocks.append((2 * mask + 1, first, swap(block, "height", 1)))
    return blocks


def mid_body(places, rows, here, local, fetched, *refs):
    blocks, (out, w_in) = refs[:-2], refs[-2:]
    d, h = here[0], here[1]
    own = d == h // 2
    w = jnp.where(own, local[0], fetched[0])
    for (mask, first), block in zip(places, blocks):
        n = block.shape[0]
        at = pl.multiple_of((h ^ mask) * rows + first, 16)
        out[pl.ds(at, n), :] = lax.dot_general(
            block[...], w, NT, preferred_element_type=F32
        ).astype(BF16)
    w_in[...] = jnp.where(own, local[1], fetched[1])


def kgrad_body(wid, group, planes, *refs):
    mids, (pre, out, pad) = refs[:planes], refs[planes:]
    cells, chans = pre.shape
    col = lax.broadcasted_iota(jnp.int32, (cells, 1), 0) % wid
    rhs = []
    for mid in mids:
        p32 = mid[...].astype(F32)
        left = jnp.where(col < wid - 1, pltpu.roll(p32, cells - 1, 0), 0.0).astype(BF16)
        right = jnp.where(col > 0, pltpu.roll(p32, 1, 0), 0.0).astype(BF16)
        rhs += [left, mid[...], right]
    rhs = jnp.concatenate(rhs, axis=1)
    lane_group = lax.broadcasted_iota(jnp.int32, (group, chans), 1) // group
    zero = jnp.zeros((wid, chans), BF16)
    pad[0:wid, :] = zero
    pad[wid + cells : 2 * wid + cells, :] = zero
    pad[wid : wid + cells, :] = jnp.maximum(pre[...], jnp.zeros((), BF16))
    for t in range(3):
        lhs = pad[t * wid : t * wid + cells, :]
        res = lax.dot_general(lhs, rhs, TN, preferred_element_type=F32)
        for p in range(planes):
            for u in range(3):
                first = (3 * p + u) * chans
                tile = res[:, first : first + chans]
                acc = jnp.zeros((group, chans), F32)
                for g in range(chans // group):
                    acc = jnp.where(lane_group == g, tile[g * group : (g + 1) * group, :], acc)
                out[p, 3 * t + u] = acc.astype(BF16)


def pair_body(here, early, late, other_early, other_late, out):
    odd = here[0] % 2
    out[1] = (early[0].astype(F32) + other_early[0].astype(F32)).astype(BF16)
    out[2 * odd] = (early[1].astype(F32) + other_late[0].astype(F32)).astype(BF16)
    out[2 - 2 * odd] = (late[0].astype(F32) + other_early[1].astype(F32)).astype(BF16)


def total_body(scale, own, other, out):
    for s in range(3):
        out[9 * s : 9 * s + 9] = (own[s].astype(F32) + other[s].astype(F32)) * scale


def back_body(wid, here, mid, near, far, pre, weights, *refs):
    outs, pad = refs[:-1], refs[-1]
    d, h = here[0], here[1]
    cells, chans = mid.shape
    rows = cells // len(outs)
    zero = jnp.zeros((wid, chans), BF16)
    odd = d % 2 == 1
    pad[1, wid : wid + cells, :] = mid[...]
    pad[2, wid : wid + cells, :] = jnp.where(odd, near[...], far[...])
    pad[0, wid : wid + cells, :] = jnp.where(odd, far[...], near[...])
    for s in range(3):
        pad[s, 0:wid, :] = zero
        pad[s, wid + cells : 2 * wid + cells, :] = zero
    col = lax.broadcasted_iota(jnp.int32, (rows, 1), 0) % wid
    for m, out in enumerate(outs):
        first = pl.multiple_of(((h // 2) ^ m) * rows, wid)
        lhs = jnp.concatenate(
            [pad[s, pl.ds(first + (2 - t) * wid, rows), :] for s in range(3) for t in range(3)], axis=1
        )
        y = lax.dot_general(lhs, weights[...], NT, preferred_element_type=F32)
        total = y[:, chans : 2 * chans]
        total = total + jnp.where(col < wid - 1, pltpu.roll(y[:, :chans], rows - 1, 0), 0.0)
        total = total + jnp.where(col > 0, pltpu.roll(y[:, 2 * chans :], 1, 0), 0.0)
        keep = pre[pl.ds(first, rows), :].astype(F32) > 0
        out[...] = jnp.where(keep, total, 0.0).astype(BF16)


def partial_body(here, skip, *refs):
    chips = 4
    grads, ws, (own, other, lhs_ref) = refs[:chips], refs[chips:-3], refs[-3:]
    chip, core = here[1] // 2, here[1] % 2
    rows = skip.shape[0]
    for m, grad in enumerate(grads):
        lhs_ref[chip ^ m] = grad[...]
    lhs = jnp.concatenate([lhs_ref[i] for i in range(chips)], axis=1)
    part, depth = ws[0].shape[0], lhs.shape[1]
    for m, w in enumerate(ws):
        for half in range(2):
            acc = lax.dot_general(
                lhs, w[:, half * depth : (half + 1) * depth], NT, preferred_element_type=F32
            )
            at = pl.ds(pl.multiple_of((chip ^ m) * 2 * part + half * part, part), part)
            here_part = jnp.where(core == 0, acc[:rows], acc[rows:])
            there_part = jnp.where(core == 0, acc[rows:], acc[:rows])
            own[:, at] = here_part + skip[:, at].astype(F32)
            other[:, at] = there_part.astype(BF16)


def weights_body(group, kernel, out):
    chans = kernel.shape[2]
    row_group = lax.broadcasted_iota(jnp.int32, (chans, chans), 0) // group
    lane_group = lax.broadcasted_iota(jnp.int32, (chans, chans), 1) // group
    zero = jnp.zeros((chans, chans), BF16)
    for o in range(27):
        st, u = o // 3, o % 3
        tiled = jnp.concatenate([kernel[o]] * (chans // group), axis=0)
        out[u * chans : (u + 1) * chans, st * chans : (st + 1) * chans] = jnp.where(
            row_group == lane_group, tiled, zero
        )


def z_swaps(x):
    n = lax.axis_size("depth")
    between = [(i, i + 1) for i in range(1, n - 1, 2)]
    far = lax.ppermute(x, "depth", between + [(j, i) for i, j in between])
    near = swap(x, "depth", 1)
    return near, far


def fast(grad_out, pre_act, w_in, w_out, kernel):
    _, rows_here, wid, width = grad_out.shape
    _, height, _, chans = pre_act.shape
    group = kernel.shape[1]
    block = rows_here * wid
    cells = height * wid
    d, h = lax.axis_index("depth"), lax.axis_index("height")
    here = jnp.stack([d, h]).astype(jnp.int32)
    skip = grad_out.reshape(block, width)
    pre = pre_act.reshape(cells, chans)

    blocks = chip_gather(skip)
    gathered = plane_gather(blocks)
    mine = call(
        pack_body, jax.ShapeDtypeStruct((2, w_out.shape[0] // 2, width), BF16), 2, nbytes=6 * w_out.size
    )(here, w_out, w_in)
    fetched = fetch(mine)
    weights = call(
        functools.partial(weights_body, group),
        jax.ShapeDtypeStruct((3 * chans, 9 * chans), BF16),
        1,
        scalars=0,
        nbytes=54 * chans * chans,
    )(order(kernel, fetched))

    places = [(mask, first) for mask, first, _ in gathered]
    mid, w_cols = call(
        functools.partial(mid_body, places, block),
        [jax.ShapeDtypeStruct((cells, chans), BF16), jax.ShapeDtypeStruct(mine.shape[1:], BF16)],
        2 + len(places),
        flops=2 * cells * width * chans,
        nbytes=2 * cells * width,
    )(here, mine, fetched, *[b for _, _, b in gathered])

    near, far = z_swaps(mid)
    kernel_flops = 2 * 9 * chans * chans * cells
    early, late = (
        call(
            functools.partial(kgrad_body, wid, group, len(planes)),
            jax.ShapeDtypeStruct((len(planes), 9, group, chans), BF16),
            len(planes) + 1,
            scalars=0,
            scratch=[pltpu.VMEM((cells + 2 * wid, chans), BF16)],
            flops=kernel_flops * len(planes),
            nbytes=6 * cells * chans,
        )(*planes, pre)
        for planes in ((mid, near), (far,))
    )
    w_blocks = [w_cols] + [swap(w_cols, "height", 2 * m) for m in (1, 2, 3)]
    pair = call(
        pair_body,
        jax.ShapeDtypeStruct((3, 9, group, chans), BF16),
        4,
        nbytes=100 * 9 * group * chans,
    )(here, order(early, *w_blocks), late, swap(early, "depth", 1), swap(late, "depth", 1))
    total_cells = cells * lax.axis_size("depth")
    kernel_grad = call(
        functools.partial(total_body, float(total_cells) ** -0.5),
        jax.ShapeDtypeStruct((27, group, chans), F32),
        2,
        scalars=0,
        flops=SPAN,
        nbytes=24 * 9 * group * chans,
    )(pair, swap(pair, "depth", 2))

    chip_cells = 2 * block
    back = call(
        functools.partial(back_body, wid),
        [jax.ShapeDtypeStruct((chip_cells, chans), BF16)] * (cells // chip_cells),
        5,
        scratch=[pltpu.VMEM((3, cells + 2 * wid, chans), BF16)],
        flops=2 * 27 * chans * chans * cells,
        nbytes=10 * cells * chans,
    )(here, mid, near, far, pre, order(weights, early, late))
    parts = [back[0]] + [swap(b, "height", 2 * m) for m, b in enumerate(back) if m]

    own, other = call(
        partial_body,
        [jax.ShapeDtypeStruct((block, width), F32), jax.ShapeDtypeStruct((block, width), BF16)],
        1 + len(parts) + len(w_blocks),
        scratch=[pltpu.VMEM((len(parts), chip_cells, chans), BF16)],
        flops=SPAN,
        nbytes=width * width,
    )(here, order(skip, pair), *parts, *w_blocks)
    theirs = order(swap(other, "height", 1), kernel_grad)
    grad_in = (own + theirs.astype(F32)).astype(BF16)
    return grad_in.reshape(grad_out.shape), kernel_grad


def with_halo(cells, axis, dim, width):
    head = lax.slice_in_dim(cells, 0, width, axis=dim)
    tail = lax.slice_in_dim(cells, cells.shape[dim] - width, cells.shape[dim], axis=dim)
    return jnp.concatenate([shift(tail, axis, 1), cells, shift(head, axis, -1)], axis=dim)


def general(grad_out, pre_act, w_in, w_out, kernel):
    product = lax.dot_general(
        grad_out,
        lax.all_gather(w_out, "depth", axis=0, tiled=True),
        (((3,), (1,)), ((), ())),
        preferred_element_type=F32,
    )
    grad_mid = product.astype(BF16)
    grouped = lax.all_to_all(grad_mid, "height", split_axis=3, concat_axis=1, tiled=True)
    padded = with_halo(grouped, "depth", 0, 1)
    padded = jnp.pad(padded, ((0, 0), (1, 1), (1, 1), (0, 0)))
    depth_len, height_len, width_len, chans = pre_act.shape
    group = kernel.shape[1]
    groups = chans // group
    hidden = jnp.maximum(pre_act, jnp.zeros_like(pre_act)).reshape(
        depth_len, height_len, width_len, groups, group
    )
    kern = kernel.reshape(27, group, groups, group)
    back = jnp.zeros((groups, group, depth_len, height_len, width_len), F32)
    grads = []
    for s in range(3):
        windows = [
            padded[2 - s : 2 - s + depth_len, 2 - t : 2 - t + height_len, 2 - u : 2 - u + width_len, :]
            for t in range(3)
            for u in range(3)
        ]
        stacked = jnp.concatenate(windows, axis=3)
        stacked = stacked.reshape(depth_len, height_len, width_len, 9, groups, group)
        back = back + jnp.einsum(
            "dhwkgj,kigj->gidhw", stacked, kern[9 * s : 9 * s + 9], preferred_element_type=F32
        )
        grads.append(jnp.einsum("dhwkgj,dhwgi->kigj", stacked, hidden, preferred_element_type=F32))
    back = jnp.transpose(back, (2, 3, 4, 0, 1)).reshape(depth_len, height_len, width_len, chans)
    grad_pre = jnp.where(pre_act > 0, back, jnp.zeros_like(back)).astype(BF16)
    part = jnp.concatenate(grads, axis=0).reshape(27, group, chans)
    total_cells = depth_len * lax.axis_size("depth") * height_len * width_len
    scale = jnp.float32(total_cells) ** (-0.5)
    kernel_grad = lax.psum(part.astype(BF16), "depth").astype(F32) * scale
    by_height = lax.all_to_all(grad_pre, "height", split_axis=1, concat_axis=3, tiled=True)
    branch = lax.dot_general(
        by_height,
        lax.all_gather(w_in, "depth", axis=0, tiled=True),
        (((3,), (1,)), ((), ())),
        preferred_element_type=F32,
    )
    return (grad_out.astype(F32) + branch).astype(BF16), kernel_grad


def solution(mesh):
    planes, cols = mesh.shape["depth"], mesh.shape["height"]

    def shards(grad_out, pre_act, w_in, w_out, kernel):
        whole_lanes = pre_act.shape[3] == 128 and pre_act.shape[0] == 1 and grad_out.shape[0] == 1
        if cols == 8 and planes == 4 and whole_lanes:
            return fast(grad_out, pre_act, w_in, w_out, kernel)
        return general(grad_out, pre_act, w_in, w_out, kernel)

    in_specs = (
        P("depth", "height", None, None),
        P("depth", None, None, "height"),
        P("depth", None),
        P("depth", None),
        P(None, None, "height"),
    )
    out_specs = (P("depth", "height", None, None), P(None, None, "height"))
    return jax.shard_map(shards, mesh=mesh, in_specs=in_specs, out_specs=out_specs, check_vma=False)
```

```python
import functools

import jax
import jax.numpy as jnp
from jax import lax
from jax.experimental import pallas as pl
from jax.experimental.pallas import tpu as pltpu
from jax.sharding import PartitionSpec as P

F32 = jnp.float32
BF16 = jnp.bfloat16
NT = (((1,), (1,)), ((), ()))
TN = (((0,), (0,)), ((), ()))
VMEM_LIMIT = 48 * 1024 * 1024
SPAN = 1 << 35


def vmem():
    return pl.BlockSpec(memory_space=pltpu.VMEM)


def smem():
    return pl.BlockSpec(memory_space=pltpu.SMEM)


def call(body, out_shape, n_in, *, scalars=1, scratch=(), flops=0, nbytes=0):
    return pl.pallas_call(
        body,
        out_shape=out_shape,
        in_specs=[smem()] * scalars + [vmem()] * n_in,
        out_specs=jax.tree.map(lambda _: vmem(), out_shape),
        scratch_shapes=list(scratch),
        compiler_params=pltpu.CompilerParams(vmem_limit_bytes=VMEM_LIMIT),
        cost_estimate=pl.CostEstimate(flops=flops, bytes_accessed=nbytes, transcendentals=0),
    )


def swap(x, axis, mask):
    n = lax.axis_size(axis)
    return lax.ppermute(x, axis, [(i, i ^ mask) for i in range(n)])


def shift(x, axis, step):
    n = lax.axis_size(axis)
    return lax.ppermute(x, axis, [(i, i + step) for i in range(n) if 0 <= i + step < n])


def order(x, *before):
    return lax.optimization_barrier((x,) + before)[0]


CARRIERS = (
    {
        (0, 1): 0, (0, 2): 1, (0, 3): 2,
        (1, 0): 1, (1, 2): 3, (1, 3): 0,
        (2, 0): 0, (2, 1): 2, (2, 3): 3,
        (3, 0): 3, (3, 1): 1, (3, 2): 2,
    },
    {
        (0, 1): 1, (0, 2): 2, (0, 3): 0,
        (1, 0): 0, (1, 2): 1, (1, 3): 3,
        (2, 0): 3, (2, 1): 0, (2, 3): 2,
        (3, 0): 1, (3, 1): 2, (3, 2): 3,
    },
)


def pack_body(here, rows, w_in, out):
    core = here[1] % 2
    part, width = rows.shape
    out[0] = rows[...]
    lanes = width // 8
    for i in range(4):
        even = w_in[:, 2 * i * lanes : (2 * i + 1) * lanes]
        odd = w_in[:, (2 * i + 1) * lanes : (2 * i + 2) * lanes]
        block = jnp.where(core == 0, even, odd)
        for half in range(2):
            first = half * width // 2 + i * lanes
            out[1, :, first : first + lanes] = block[half * part : (half + 1) * part]


def fetch(mine):
    cols = lax.axis_size("height")
    pairs = [
        (src * cols + 2 * chip + c, dst * cols + 2 * src + c)
        for c, carrier in enumerate(CARRIERS)
        for (src, dst), chip in carrier.items()
    ]
    return lax.ppermute(mine, ("depth", "height"), pairs)


def chip_gather(x):
    half = x.shape[0] // 2
    across_x, across_y = swap(x, "height", 2), swap(x, "height", 4)
    diag_a = swap(across_x[:half], "height", 4)
    diag_b = swap(across_y[half:], "height", 2)
    return [(0, 0, x), (1, 0, across_x), (2, 0, across_y), (3, 0, diag_a), (3, half, diag_b)]


def plane_gather(chip_blocks):
    blocks = []
    for mask, first, block in chip_blocks:
        blocks.append((2 * mask, first, block))
        blocks.append((2 * mask + 1, first, swap(block, "height", 1)))
    return blocks


def mid_body(places, rows, here, local, fetched, *refs):
    blocks, (out, w_in) = refs[:-2], refs[-2:]
    d, h = here[0], here[1]
    own = d == h // 2
    w = jnp.where(own, local[0], fetched[0])
    for (mask, first), block in zip(places, blocks):
        n = block.shape[0]
        at = pl.multiple_of((h ^ mask) * rows + first, 16)
        out[pl.ds(at, n), :] = lax.dot_general(
            block[...], w, NT, preferred_element_type=F32
        ).astype(BF16)
    w_in[...] = jnp.where(own, local[1], fetched[1])


def kgrad_body(wid, group, planes, *refs):
    mids, (pre, out, pad) = refs[:planes], refs[planes:]
    cells, chans = pre.shape
    col = lax.broadcasted_iota(jnp.int32, (cells, 1), 0) % wid
    rhs = []
    for mid in mids:
        p32 = mid[...].astype(F32)
        left = jnp.where(col < wid - 1, pltpu.roll(p32, cells - 1, 0), 0.0).astype(BF16)
        right = jnp.where(col > 0, pltpu.roll(p32, 1, 0), 0.0).astype(BF16)
        rhs += [left, mid[...], right]
    rhs = jnp.concatenate(rhs, axis=1)
    lane_group = lax.broadcasted_iota(jnp.int32, (group, chans), 1) // group
    zero = jnp.zeros((wid, chans), BF16)
    pad[0:wid, :] = zero
    pad[wid + cells : 2 * wid + cells, :] = zero
    pad[wid : wid + cells, :] = jnp.maximum(pre[...], jnp.zeros((), BF16))
    for t in range(3):
        lhs = pad[t * wid : t * wid + cells, :]
        res = lax.dot_general(lhs, rhs, TN, preferred_element_type=F32)
        for p in range(planes):
            for u in range(3):
                first = (3 * p + u) * chans
                tile = res[:, first : first + chans]
                acc = jnp.zeros((group, chans), F32)
                for g in range(chans // group):
                    acc = jnp.where(lane_group == g, tile[g * group : (g + 1) * group, :], acc)
                out[p, 3 * t + u] = acc.astype(BF16)


def pair_body(here, early, late, other_early, other_late, out):
    odd = here[0] % 2
    out[1] = (early[0].astype(F32) + other_early[0].astype(F32)).astype(BF16)
    out[2 * odd] = (early[1].astype(F32) + other_late[0].astype(F32)).astype(BF16)
    out[2 - 2 * odd] = (late[0].astype(F32) + other_early[1].astype(F32)).astype(BF16)


def total_body(scale, own, other, out):
    for s in range(3):
        out[9 * s : 9 * s + 9] = (own[s].astype(F32) + other[s].astype(F32)) * scale


def back_body(wid, here, mid, near, far, pre, weights, *refs):
    outs, pad = refs[:-1], refs[-1]
    d, h = here[0], here[1]
    cells, chans = mid.shape
    rows = cells // len(outs)
    zero = jnp.zeros((wid, chans), BF16)
    odd = d % 2 == 1
    pad[1, wid : wid + cells, :] = mid[...]
    pad[2, wid : wid + cells, :] = jnp.where(odd, near[...], far[...])
    pad[0, wid : wid + cells, :] = jnp.where(odd, far[...], near[...])
    for s in range(3):
        pad[s, 0:wid, :] = zero
        pad[s, wid + cells : 2 * wid + cells, :] = zero
    col = lax.broadcasted_iota(jnp.int32, (rows, 1), 0) % wid
    for m, out in enumerate(outs):
        first = pl.multiple_of(((h // 2) ^ m) * rows, wid)
        lhs = jnp.concatenate(
            [pad[s, pl.ds(first + (2 - t) * wid, rows), :] for s in range(3) for t in range(3)], axis=1
        )
        y = lax.dot_general(lhs, weights[...], NT, preferred_element_type=F32)
        total = y[:, chans : 2 * chans]
        total = total + jnp.where(col < wid - 1, pltpu.roll(y[:, :chans], rows - 1, 0), 0.0)
        total = total + jnp.where(col > 0, pltpu.roll(y[:, 2 * chans :], 1, 0), 0.0)
        keep = pre[pl.ds(first, rows), :].astype(F32) > 0
        out[...] = jnp.where(keep, total, 0.0).astype(BF16)


def partial_body(here, skip, *refs):
    chips = 4
    grads, ws, (own, other, lhs_ref) = refs[:chips], refs[chips:-3], refs[-3:]
    chip, core = here[1] // 2, here[1] % 2
    rows = skip.shape[0]
    for m, grad in enumerate(grads):
        lhs_ref[chip ^ m] = grad[...]
    lhs = jnp.concatenate([lhs_ref[i] for i in range(chips)], axis=1)
    part, depth = ws[0].shape[0], lhs.shape[1]
    for m, w in enumerate(ws):
        for half in range(2):
            acc = lax.dot_general(
                lhs, w[:, half * depth : (half + 1) * depth], NT, preferred_element_type=F32
            )
            at = pl.ds(pl.multiple_of((chip ^ m) * 2 * part + half * part, part), part)
            here_part = jnp.where(core == 0, acc[:rows], acc[rows:])
            there_part = jnp.where(core == 0, acc[rows:], acc[:rows])
            own[:, at] = here_part + skip[:, at].astype(F32)
            other[:, at] = there_part.astype(BF16)


def weights_body(group, kernel, out):
    chans = kernel.shape[2]
    row_group = lax.broadcasted_iota(jnp.int32, (chans, chans), 0) // group
    lane_group = lax.broadcasted_iota(jnp.int32, (chans, chans), 1) // group
    zero = jnp.zeros((chans, chans), BF16)
    for o in range(27):
        st, u = o // 3, o % 3
        tiled = jnp.concatenate([kernel[o]] * (chans // group), axis=0)
        out[u * chans : (u + 1) * chans, st * chans : (st + 1) * chans] = jnp.where(
            row_group == lane_group, tiled, zero
        )


def z_swaps(x):
    n = lax.axis_size("depth")
    between = [(i, i + 1) for i in range(1, n - 1, 2)]
    far = lax.ppermute(x, "depth", between + [(j, i) for i, j in between])
    near = swap(x, "depth", 1)
    return near, far


def fast(grad_out, pre_act, w_in, w_out, kernel):
    _, rows_here, wid, width = grad_out.shape
    _, height, _, chans = pre_act.shape
    group = kernel.shape[1]
    block = rows_here * wid
    cells = height * wid
    d, h = lax.axis_index("depth"), lax.axis_index("height")
    here = jnp.stack([d, h]).astype(jnp.int32)
    skip = grad_out.reshape(block, width)
    pre = pre_act.reshape(cells, chans)

    blocks = chip_gather(skip)
    gathered = plane_gather(blocks)
    part = w_out.shape[0] // 2
    rows = lax.dynamic_slice_in_dim(w_out, h % 2 * part, part, axis=0)
    mine = call(
        pack_body, jax.ShapeDtypeStruct((2, part, width), BF16), 2, nbytes=6 * w_out.size
    )(here, rows, w_in)
    fetched = fetch(mine)
    weights = call(
        functools.partial(weights_body, group),
        jax.ShapeDtypeStruct((3 * chans, 9 * chans), BF16),
        1,
        scalars=0,
        nbytes=54 * chans * chans,
    )(order(kernel, fetched))

    places = [(mask, first) for mask, first, _ in gathered]
    mid, w_cols = call(
        functools.partial(mid_body, places, block),
        [jax.ShapeDtypeStruct((cells, chans), BF16), jax.ShapeDtypeStruct(mine.shape[1:], BF16)],
        2 + len(places),
        flops=2 * cells * width * chans,
        nbytes=2 * cells * width,
    )(here, mine, fetched, *[b for _, _, b in gathered])

    near, far = z_swaps(mid)
    kernel_flops = 2 * 9 * chans * chans * cells
    early, late = (
        call(
            functools.partial(kgrad_body, wid, group, len(planes)),
            jax.ShapeDtypeStruct((len(planes), 9, group, chans), BF16),
            len(planes) + 1,
            scalars=0,
            scratch=[pltpu.VMEM((cells + 2 * wid, chans), BF16)],
            flops=kernel_flops * len(planes),
            nbytes=6 * cells * chans,
        )(*planes, pre)
        for planes in ((mid, near), (far,))
    )
    w_blocks = [w_cols] + [swap(w_cols, "height", 2 * m) for m in (1, 2)]
    w_blocks.append(swap(order(w_cols, late), "height", 6))
    chip_cells = 2 * block
    back = call(
        functools.partial(back_body, wid),
        [jax.ShapeDtypeStruct((chip_cells, chans), BF16)] * (cells // chip_cells),
        5,
        scratch=[pltpu.VMEM((3, cells + 2 * wid, chans), BF16)],
        flops=2 * 27 * chans * chans * cells,
        nbytes=10 * cells * chans,
    )(here, mid, near, far, pre, order(weights, early, late))
    pair = call(
        pair_body,
        jax.ShapeDtypeStruct((3, 9, group, chans), BF16),
        4,
        nbytes=100 * 9 * group * chans,
    )(here, order(early, back[0], w_blocks[1], w_blocks[2]), late, swap(early, "depth", 1), swap(late, "depth", 1))
    total_cells = cells * lax.axis_size("depth")
    other_pair = swap(pair, "depth", 2)
    kernel_grad = call(
        functools.partial(total_body, float(total_cells) ** -0.5),
        jax.ShapeDtypeStruct((27, group, chans), F32),
        2,
        scalars=0,
        flops=SPAN,
        nbytes=24 * 9 * group * chans,
    )(pair, other_pair)

    parts = [back[0]] + [swap(b, "height", 2 * m) for m, b in enumerate(back) if m]

    own, other = call(
        partial_body,
        [jax.ShapeDtypeStruct((block, width), F32), jax.ShapeDtypeStruct((block, width), BF16)],
        1 + len(parts) + len(w_blocks),
        scratch=[pltpu.VMEM((len(parts), chip_cells, chans), BF16)],
        flops=2 * block * width * width,
        nbytes=width * width,
    )(here, order(skip, pair), *parts, *w_blocks)
    theirs = swap(other, "height", 1)
    theirs = order(theirs, kernel_grad)
    grad_in = (own + theirs.astype(F32)).astype(BF16)
    return grad_in.reshape(grad_out.shape), kernel_grad


def with_halo(cells, axis, dim, width):
    head = lax.slice_in_dim(cells, 0, width, axis=dim)
    tail = lax.slice_in_dim(cells, cells.shape[dim] - width, cells.shape[dim], axis=dim)
    return jnp.concatenate([shift(tail, axis, 1), cells, shift(head, axis, -1)], axis=dim)


def general(grad_out, pre_act, w_in, w_out, kernel):
    product = lax.dot_general(
        grad_out,
        lax.all_gather(w_out, "depth", axis=0, tiled=True),
        (((3,), (1,)), ((), ())),
        preferred_element_type=F32,
    )
    grad_mid = product.astype(BF16)
    grouped = lax.all_to_all(grad_mid, "height", split_axis=3, concat_axis=1, tiled=True)
    padded = with_halo(grouped, "depth", 0, 1)
    padded = jnp.pad(padded, ((0, 0), (1, 1), (1, 1), (0, 0)))
    depth_len, height_len, width_len, chans = pre_act.shape
    group = kernel.shape[1]
    groups = chans // group
    hidden = jnp.maximum(pre_act, jnp.zeros_like(pre_act)).reshape(
        depth_len, height_len, width_len, groups, group
    )
    kern = kernel.reshape(27, group, groups, group)
    back = jnp.zeros((groups, group, depth_len, height_len, width_len), F32)
    grads = []
    for s in range(3):
        windows = [
            padded[2 - s : 2 - s + depth_len, 2 - t : 2 - t + height_len, 2 - u : 2 - u + width_len, :]
            for t in range(3)
            for u in range(3)
        ]
        stacked = jnp.concatenate(windows, axis=3)
        stacked = stacked.reshape(depth_len, height_len, width_len, 9, groups, group)
        back = back + jnp.einsum(
            "dhwkgj,kigj->gidhw", stacked, kern[9 * s : 9 * s + 9], preferred_element_type=F32
        )
        grads.append(jnp.einsum("dhwkgj,dhwgi->kigj", stacked, hidden, preferred_element_type=F32))
    back = jnp.transpose(back, (2, 3, 4, 0, 1)).reshape(depth_len, height_len, width_len, chans)
    grad_pre = jnp.where(pre_act > 0, back, jnp.zeros_like(back)).astype(BF16)
    part = jnp.concatenate(grads, axis=0).reshape(27, group, chans)
    total_cells = depth_len * lax.axis_size("depth") * height_len * width_len
    scale = jnp.float32(total_cells) ** (-0.5)
    kernel_grad = lax.psum(part.astype(BF16), "depth").astype(F32) * scale
    by_height = lax.all_to_all(grad_pre, "height", split_axis=1, concat_axis=3, tiled=True)
    branch = lax.dot_general(
        by_height,
        lax.all_gather(w_in, "depth", axis=0, tiled=True),
        (((3,), (1,)), ((), ())),
        preferred_element_type=F32,
    )
    return (grad_out.astype(F32) + branch).astype(BF16), kernel_grad


def solution(mesh):
    planes, cols = mesh.shape["depth"], mesh.shape["height"]

    def shards(grad_out, pre_act, w_in, w_out, kernel):
        whole_lanes = pre_act.shape[3] == 128 and pre_act.shape[0] == 1 and grad_out.shape[0] == 1
        if cols == 8 and planes == 4 and whole_lanes:
            return fast(grad_out, pre_act, w_in, w_out, kernel)
        return general(grad_out, pre_act, w_in, w_out, kernel)

    in_specs = (
        P("depth", "height", None, None),
        P("depth", None, None, "height"),
        P("depth", None),
        P("depth", None),
        P(None, None, "height"),
    )
    out_specs = (P("depth", "height", None, None), P(None, None, "height"))
    return jax.shard_map(shards, mesh=mesh, in_specs=in_specs, out_specs=out_specs, check_vma=False)
```

```python
import functools

import jax
import jax.numpy as jnp
from jax import lax
from jax.experimental import pallas as pl
from jax.experimental.pallas import tpu as pltpu
from jax.sharding import PartitionSpec as P

F32 = jnp.float32
BF16 = jnp.bfloat16
NT = (((1,), (1,)), ((), ()))
TN = (((0,), (0,)), ((), ()))
VMEM_LIMIT = 48 * 1024 * 1024
SPAN = 1 << 35


def vmem():
    return pl.BlockSpec(memory_space=pltpu.VMEM)


def smem():
    return pl.BlockSpec(memory_space=pltpu.SMEM)


def call(body, out_shape, n_in, *, scalars=1, scratch=(), flops=0, nbytes=0):
    return pl.pallas_call(
        body,
        out_shape=out_shape,
        in_specs=[smem()] * scalars + [vmem()] * n_in,
        out_specs=jax.tree.map(lambda _: vmem(), out_shape),
        scratch_shapes=list(scratch),
        compiler_params=pltpu.CompilerParams(vmem_limit_bytes=VMEM_LIMIT),
        cost_estimate=pl.CostEstimate(flops=flops, bytes_accessed=nbytes, transcendentals=0),
    )


def swap(x, axis, mask):
    n = lax.axis_size(axis)
    return lax.ppermute(x, axis, [(i, i ^ mask) for i in range(n)])


def shift(x, axis, step):
    n = lax.axis_size(axis)
    return lax.ppermute(x, axis, [(i, i + step) for i in range(n) if 0 <= i + step < n])


def order(x, *before):
    return lax.optimization_barrier((x,) + before)[0]


CARRIERS = (
    {
        (0, 1): 1, (0, 2): 0, (0, 3): 2,
        (1, 0): 0, (1, 2): 3, (1, 3): 1,
        (2, 0): 2, (2, 1): 0, (2, 3): 3,
        (3, 0): 1, (3, 1): 3, (3, 2): 2,
    },
    {
        (0, 1): 0, (0, 2): 2, (0, 3): 1,
        (1, 0): 1, (1, 2): 0, (1, 3): 3,
        (2, 0): 0, (2, 1): 3, (2, 3): 2,
        (3, 0): 2, (3, 1): 1, (3, 2): 3,
    },
)


def pack_body(here, rows, w_in, out):
    core = here[1] % 2
    part, width = rows.shape
    out[0] = rows[...]
    lanes = width // 8
    for i in range(4):
        even = w_in[:, 2 * i * lanes : (2 * i + 1) * lanes]
        odd = w_in[:, (2 * i + 1) * lanes : (2 * i + 2) * lanes]
        block = jnp.where(core == 0, even, odd)
        for half in range(2):
            first = half * width // 2 + i * lanes
            out[1, :, first : first + lanes] = block[half * part : (half + 1) * part]


def fetch(mine):
    cols = lax.axis_size("height")
    pairs = [
        (src * cols + 2 * chip + c, dst * cols + 2 * src + c)
        for c, carrier in enumerate(CARRIERS)
        for (src, dst), chip in carrier.items()
    ]
    return lax.ppermute(mine, ("depth", "height"), pairs)


def chip_gather(x):
    half = x.shape[0] // 2
    across_x, across_y = swap(x, "height", 2), swap(x, "height", 4)
    diag_a = swap(across_x[:half], "height", 4)
    diag_b = swap(across_y[half:], "height", 2)
    return [(0, 0, x), (1, 0, across_x), (2, 0, across_y), (3, 0, diag_a), (3, half, diag_b)]


def plane_gather(chip_blocks):
    blocks = []
    for mask, first, block in chip_blocks:
        blocks.append((2 * mask, first, block))
        blocks.append((2 * mask + 1, first, swap(block, "height", 1)))
    return blocks


def mid_body(places, rows, here, local, fetched, *refs):
    blocks, out = refs[:-1], refs[-1]
    d, h = here[0], here[1]
    w = jnp.where(d == h // 2, local[0], fetched[0])
    lhs = jnp.concatenate([block[...] for block in blocks], axis=0)
    mid = lax.dot_general(lhs, w, NT, preferred_element_type=F32).astype(BF16)
    start = 0
    for (mask, first), block in zip(places, blocks):
        n = block.shape[0]
        at = pl.multiple_of((h ^ mask) * rows + first, 16)
        out[pl.ds(at, n), :] = mid[start : start + n]
        start += n


def columns_body(here, local, fetched, out):
    packed = jnp.where(here[0] == here[1] // 2, local[1], fetched[1])
    part, width = packed.shape[0], packed.shape[1] // 2
    out[:part] = packed[:, :width]
    out[part:] = packed[:, width:]


def kgrad_body(wid, group, planes, *refs):
    mids, (pre, out, pad) = refs[:planes], refs[planes:]
    cells, chans = pre.shape
    col = lax.broadcasted_iota(jnp.int32, (cells, 1), 0) % wid
    rhs = []
    for mid in mids:
        p32 = mid[...].astype(F32)
        left = jnp.where(col < wid - 1, pltpu.roll(p32, cells - 1, 0), 0.0).astype(BF16)
        right = jnp.where(col > 0, pltpu.roll(p32, 1, 0), 0.0).astype(BF16)
        rhs += [left, mid[...], right]
    rhs = jnp.concatenate(rhs, axis=1)
    lane_group = lax.broadcasted_iota(jnp.int32, (group, chans), 1) // group
    zero = jnp.zeros((wid, chans), BF16)
    pad[0:wid, :] = zero
    pad[wid + cells : 2 * wid + cells, :] = zero
    pad[wid : wid + cells, :] = jnp.maximum(pre[...], jnp.zeros((), BF16))
    for t in range(3):
        lhs = pad[t * wid : t * wid + cells, :]
        res = lax.dot_general(lhs, rhs, TN, preferred_element_type=F32)
        for p in range(planes):
            for u in range(3):
                first = (3 * p + u) * chans
                tile = res[:, first : first + chans]
                acc = jnp.zeros((group, chans), F32)
                for g in range(chans // group):
                    acc = jnp.where(lane_group == g, tile[g * group : (g + 1) * group, :], acc)
                out[p, 3 * t + u] = acc.astype(BF16)


def pair_body(here, early, late, other_early, other_late, out):
    odd = here[0] % 2
    out[1] = (early[0].astype(F32) + other_early[0].astype(F32)).astype(BF16)
    out[2 * odd] = (early[1].astype(F32) + other_late[0].astype(F32)).astype(BF16)
    out[2 - 2 * odd] = (late[0].astype(F32) + other_early[1].astype(F32)).astype(BF16)


def total_body(scale, own, other, out):
    for s in range(3):
        out[9 * s : 9 * s + 9] = (own[s].astype(F32) + other[s].astype(F32)) * scale


def back_body(wid, here, mid, near, far, pre, weights, *refs):
    outs, pad = refs[:-1], refs[-1]
    d, h = here[0], here[1]
    cells, chans = mid.shape
    rows = cells // len(outs)
    zero = jnp.zeros((wid, chans), BF16)
    odd = d % 2 == 1
    pad[1, wid : wid + cells, :] = mid[...]
    pad[2, wid : wid + cells, :] = jnp.where(odd, near[...], far[...])
    pad[0, wid : wid + cells, :] = jnp.where(odd, far[...], near[...])
    for s in range(3):
        pad[s, 0:wid, :] = zero
        pad[s, wid + cells : 2 * wid + cells, :] = zero
    col = lax.broadcasted_iota(jnp.int32, (2 * rows, 1), 0) % wid
    chip = h // 2
    for m in range(0, len(outs), 2):
        first = pl.multiple_of(((chip ^ m) // 2) * 2 * rows, wid)
        lhs = jnp.concatenate(
            [pad[s, pl.ds(first + (2 - t) * wid, 2 * rows), :] for s in range(3) for t in range(3)], axis=1
        )
        y = lax.dot_general(lhs, weights[...], NT, preferred_element_type=F32)
        total = y[:, chans : 2 * chans]
        total = total + jnp.where(col < wid - 1, pltpu.roll(y[:, :chans], 2 * rows - 1, 0), 0.0)
        total = total + jnp.where(col > 0, pltpu.roll(y[:, 2 * chans :], 1, 0), 0.0)
        keep = pre[pl.ds(first, 2 * rows), :].astype(F32) > 0
        total = jnp.where(keep, total, 0.0).astype(BF16)
        even = chip % 2 == 0
        outs[m][...] = jnp.where(even, total[:rows], total[rows:])
        outs[m + 1][...] = jnp.where(even, total[rows:], total[:rows])


def partial_body(here, skip, *refs):
    chips = 4
    grads, ws, (own, other, lhs_ref) = refs[:chips], refs[chips:-3], refs[-3:]
    chip, core = here[1] // 2, here[1] % 2
    rows = skip.shape[0]
    for m, grad in enumerate(grads):
        lhs_ref[chip ^ m] = grad[...]
    lhs = jnp.concatenate([lhs_ref[i] for i in range(chips)], axis=1)
    for m, w in enumerate(ws):
        acc = lax.dot_general(lhs, w[...], NT, preferred_element_type=F32)
        width = w.shape[0]
        at = pl.ds(pl.multiple_of((chip ^ m) * width, width), width)
        here_part = jnp.where(core == 0, acc[:rows], acc[rows:])
        there_part = jnp.where(core == 0, acc[rows:], acc[:rows])
        own[:, at] = here_part + skip[:, at].astype(F32)
        other[:, at] = there_part.astype(BF16)


def weights_body(group, kernel, out):
    chans = kernel.shape[2]
    row_group = lax.broadcasted_iota(jnp.int32, (chans, chans), 0) // group
    lane_group = lax.broadcasted_iota(jnp.int32, (chans, chans), 1) // group
    zero = jnp.zeros((chans, chans), BF16)
    for o in range(27):
        st, u = o // 3, o % 3
        tiled = jnp.concatenate([kernel[o]] * (chans // group), axis=0)
        out[u * chans : (u + 1) * chans, st * chans : (st + 1) * chans] = jnp.where(
            row_group == lane_group, tiled, zero
        )


def z_swaps(x):
    n = lax.axis_size("depth")
    between = [(i, i + 1) for i in range(1, n - 1, 2)]
    far = lax.ppermute(x, "depth", between + [(j, i) for i, j in between])
    near = swap(x, "depth", 1)
    return near, far


def fast(grad_out, pre_act, w_in, w_out, kernel):
    _, rows_here, wid, width = grad_out.shape
    _, height, _, chans = pre_act.shape
    group = kernel.shape[1]
    block = rows_here * wid
    cells = height * wid
    d, h = lax.axis_index("depth"), lax.axis_index("height")
    here = jnp.stack([d, h]).astype(jnp.int32)
    skip = grad_out.reshape(block, width)
    pre = pre_act.reshape(cells, chans)

    blocks = chip_gather(skip)
    gathered = plane_gather(blocks)
    part = w_out.shape[0] // 2
    rows = lax.dynamic_slice_in_dim(w_out, h % 2 * part, part, axis=0)
    mine = call(
        pack_body, jax.ShapeDtypeStruct((2, part, width), BF16), 2, nbytes=6 * w_out.size
    )(here, rows, w_in)
    fetched = fetch(mine)
    weights = call(
        functools.partial(weights_body, group),
        jax.ShapeDtypeStruct((3 * chans, 9 * chans), BF16),
        1,
        scalars=0,
        nbytes=54 * chans * chans,
    )(order(kernel, fetched))

    places = [(mask, first) for mask, first, _ in gathered]
    mid = call(
        functools.partial(mid_body, places, block),
        jax.ShapeDtypeStruct((cells, chans), BF16),
        2 + len(places),
        flops=2 * cells * width * chans,
        nbytes=2 * cells * width,
    )(here, mine, fetched, *[b for _, _, b in gathered])

    near, far = z_swaps(mid)
    w_cols = call(
        columns_body, jax.ShapeDtypeStruct((w_in.shape[0], width // 2), BF16), 2, nbytes=2 * w_in.size
    )(here, order(mine, mid), fetched)
    kernel_flops = 2 * 9 * chans * chans * cells
    early, late = (
        call(
            functools.partial(kgrad_body, wid, group, len(planes)),
            jax.ShapeDtypeStruct((len(planes), 9, group, chans), BF16),
            len(planes) + 1,
            scalars=0,
            scratch=[pltpu.VMEM((cells + 2 * wid, chans), BF16)],
            flops=kernel_flops * len(planes),
            nbytes=6 * cells * chans,
        )(*planes, pre)
        for planes in ((mid, near), (far,))
    )
    w_blocks = [w_cols] + [swap(w_cols, "height", 2 * m) for m in (1, 2)]
    w_blocks.append(swap(order(w_cols, late), "height", 6))
    chip_cells = 2 * block
    back = call(
        functools.partial(back_body, wid),
        [jax.ShapeDtypeStruct((chip_cells, chans), BF16)] * (cells // chip_cells),
        5,
        scratch=[pltpu.VMEM((3, cells + 2 * wid, chans), BF16)],
        flops=2 * 27 * chans * chans * cells,
        nbytes=10 * cells * chans,
    )(here, mid, near, far, pre, order(weights, early, late))
    pair = call(
        pair_body,
        jax.ShapeDtypeStruct((3, 9, group, chans), BF16),
        4,
        nbytes=100 * 9 * group * chans,
    )(here, order(early, back[0], w_blocks[1], w_blocks[2]), late, swap(early, "depth", 1), swap(late, "depth", 1))
    total_cells = cells * lax.axis_size("depth")
    other_pair = swap(pair, "depth", 2)
    kernel_grad = call(
        functools.partial(total_body, float(total_cells) ** -0.5),
        jax.ShapeDtypeStruct((27, group, chans), F32),
        2,
        scalars=0,
        flops=SPAN,
        nbytes=24 * 9 * group * chans,
    )(pair, other_pair)

    parts = [back[0]] + [swap(b, "height", 2 * m) for m, b in enumerate(back) if m]

    own, other = call(
        partial_body,
        [jax.ShapeDtypeStruct((block, width), F32), jax.ShapeDtypeStruct((block, width), BF16)],
        1 + len(parts) + len(w_blocks),
        scratch=[pltpu.VMEM((len(parts), chip_cells, chans), BF16)],
        flops=2 * block * width * width,
        nbytes=width * width,
    )(here, order(skip, pair), *parts, *w_blocks)
    theirs = swap(other, "height", 1)
    theirs = order(theirs, kernel_grad)
    grad_in = (own + theirs.astype(F32)).astype(BF16)
    return grad_in.reshape(grad_out.shape), kernel_grad


def with_halo(cells, axis, dim, width):
    head = lax.slice_in_dim(cells, 0, width, axis=dim)
    tail = lax.slice_in_dim(cells, cells.shape[dim] - width, cells.shape[dim], axis=dim)
    return jnp.concatenate([shift(tail, axis, 1), cells, shift(head, axis, -1)], axis=dim)


def general(grad_out, pre_act, w_in, w_out, kernel):
    product = lax.dot_general(
        grad_out,
        lax.all_gather(w_out, "depth", axis=0, tiled=True),
        (((3,), (1,)), ((), ())),
        preferred_element_type=F32,
    )
    grad_mid = product.astype(BF16)
    grouped = lax.all_to_all(grad_mid, "height", split_axis=3, concat_axis=1, tiled=True)
    padded = with_halo(grouped, "depth", 0, 1)
    padded = jnp.pad(padded, ((0, 0), (1, 1), (1, 1), (0, 0)))
    depth_len, height_len, width_len, chans = pre_act.shape
    group = kernel.shape[1]
    groups = chans // group
    hidden = jnp.maximum(pre_act, jnp.zeros_like(pre_act)).reshape(
        depth_len, height_len, width_len, groups, group
    )
    kern = kernel.reshape(27, group, groups, group)
    back = jnp.zeros((groups, group, depth_len, height_len, width_len), F32)
    grads = []
    for s in range(3):
        windows = [
            padded[2 - s : 2 - s + depth_len, 2 - t : 2 - t + height_len, 2 - u : 2 - u + width_len, :]
            for t in range(3)
            for u in range(3)
        ]
        stacked = jnp.concatenate(windows, axis=3)
        stacked = stacked.reshape(depth_len, height_len, width_len, 9, groups, group)
        back = back + jnp.einsum(
            "dhwkgj,kigj->gidhw", stacked, kern[9 * s : 9 * s + 9], preferred_element_type=F32
        )
        grads.append(jnp.einsum("dhwkgj,dhwgi->kigj", stacked, hidden, preferred_element_type=F32))
    back = jnp.transpose(back, (2, 3, 4, 0, 1)).reshape(depth_len, height_len, width_len, chans)
    grad_pre = jnp.where(pre_act > 0, back, jnp.zeros_like(back)).astype(BF16)
    part = jnp.concatenate(grads, axis=0).reshape(27, group, chans)
    total_cells = depth_len * lax.axis_size("depth") * height_len * width_len
    scale = jnp.float32(total_cells) ** (-0.5)
    kernel_grad = lax.psum(part.astype(BF16), "depth").astype(F32) * scale
    by_height = lax.all_to_all(grad_pre, "height", split_axis=1, concat_axis=3, tiled=True)
    branch = lax.dot_general(
        by_height,
        lax.all_gather(w_in, "depth", axis=0, tiled=True),
        (((3,), (1,)), ((), ())),
        preferred_element_type=F32,
    )
    return (grad_out.astype(F32) + branch).astype(BF16), kernel_grad


def solution(mesh):
    planes, cols = mesh.shape["depth"], mesh.shape["height"]

    def shards(grad_out, pre_act, w_in, w_out, kernel):
        whole_lanes = pre_act.shape[3] == 128 and pre_act.shape[0] == 1 and grad_out.shape[0] == 1
        if cols == 8 and planes == 4 and whole_lanes:
            return fast(grad_out, pre_act, w_in, w_out, kernel)
        return general(grad_out, pre_act, w_in, w_out, kernel)

    in_specs = (
        P("depth", "height", None, None),
        P("depth", None, None, "height"),
        P("depth", None),
        P("depth", None),
        P(None, None, "height"),
    )
    out_specs = (P("depth", "height", None, None), P(None, None, "height"))
    return jax.shard_map(shards, mesh=mesh, in_specs=in_specs, out_specs=out_specs, check_vma=False)
```

```python
import functools

import jax
import jax.numpy as jnp
from jax import lax
from jax.experimental import pallas as pl
from jax.experimental.pallas import tpu as pltpu
from jax.sharding import PartitionSpec as P

F32 = jnp.float32
BF16 = jnp.bfloat16
NT = (((1,), (1,)), ((), ()))
TN = (((0,), (0,)), ((), ()))
VMEM_LIMIT = 48 * 1024 * 1024
SPAN = 1 << 35


def vmem():
    return pl.BlockSpec(memory_space=pltpu.VMEM)


def smem():
    return pl.BlockSpec(memory_space=pltpu.SMEM)


def call(body, out_shape, n_in, *, scalars=1, scratch=(), flops=0, nbytes=0):
    return pl.pallas_call(
        body,
        out_shape=out_shape,
        in_specs=[smem()] * scalars + [vmem()] * n_in,
        out_specs=jax.tree.map(lambda _: vmem(), out_shape),
        scratch_shapes=list(scratch),
        compiler_params=pltpu.CompilerParams(vmem_limit_bytes=VMEM_LIMIT),
        cost_estimate=pl.CostEstimate(flops=flops, bytes_accessed=nbytes, transcendentals=0),
    )


def swap(x, axis, mask):
    n = lax.axis_size(axis)
    return lax.ppermute(x, axis, [(i, i ^ mask) for i in range(n)])


def shift(x, axis, step):
    n = lax.axis_size(axis)
    return lax.ppermute(x, axis, [(i, i + step) for i in range(n) if 0 <= i + step < n])


def order(x, *before):
    return lax.optimization_barrier((x,) + before)[0]


CARRIERS = (
    {
        (0, 1): 1, (0, 2): 0, (0, 3): 2,
        (1, 0): 0, (1, 2): 3, (1, 3): 1,
        (2, 0): 2, (2, 1): 0, (2, 3): 3,
        (3, 0): 1, (3, 1): 3, (3, 2): 2,
    },
    {
        (0, 1): 0, (0, 2): 2, (0, 3): 1,
        (1, 0): 1, (1, 2): 0, (1, 3): 3,
        (2, 0): 0, (2, 1): 3, (2, 3): 2,
        (3, 0): 2, (3, 1): 1, (3, 2): 3,
    },
)


def pack_body(here, rows, w_in, out):
    core = here[1] % 2
    part, width = rows.shape
    out[0] = rows[...]
    lanes = width // 8
    for i in range(4):
        even = w_in[:, 2 * i * lanes : (2 * i + 1) * lanes]
        odd = w_in[:, (2 * i + 1) * lanes : (2 * i + 2) * lanes]
        block = jnp.where(core == 0, even, odd)
        for half in range(2):
            first = half * width // 2 + i * lanes
            out[1, :, first : first + lanes] = block[half * part : (half + 1) * part]


def fetch(mine):
    cols = lax.axis_size("height")
    pairs = [
        (src * cols + 2 * chip + c, dst * cols + 2 * src + c)
        for c, carrier in enumerate(CARRIERS)
        for (src, dst), chip in carrier.items()
    ]
    return lax.ppermute(mine, ("depth", "height"), pairs)


def chip_gather(x):
    half = x.shape[0] // 2
    across_x, across_y = swap(x, "height", 2), swap(x, "height", 4)
    diag_a = swap(across_x[:half], "height", 4)
    diag_b = swap(across_y[half:], "height", 2)
    return [(0, 0, x), (1, 0, across_x), (2, 0, across_y), (3, 0, diag_a), (3, half, diag_b)]


def plane_gather(chip_blocks):
    blocks = []
    for mask, first, block in chip_blocks:
        blocks.append((2 * mask, first, block))
        blocks.append((2 * mask + 1, first, swap(block, "height", 1)))
    return blocks


def mid_body(places, rows, here, local, fetched, *refs):
    blocks, out = refs[:-1], refs[-1]
    d, h = here[0], here[1]
    w = jnp.where(d == h // 2, local[0], fetched[0])
    lhs = jnp.concatenate([block[...] for block in blocks], axis=0)
    mid = lax.dot_general(lhs, w, NT, preferred_element_type=F32).astype(BF16)
    start = 0
    for (mask, first), block in zip(places, blocks):
        n = block.shape[0]
        at = pl.multiple_of((h ^ mask) * rows + first, 16)
        out[pl.ds(at, n), :] = mid[start : start + n]
        start += n


def columns_body(here, local, fetched, out):
    packed = jnp.where(here[0] == here[1] // 2, local[1], fetched[1])
    part, width = packed.shape[0], packed.shape[1] // 2
    out[:part] = packed[:, :width]
    out[part:] = packed[:, width:]


def kgrad_body(wid, group, planes, *refs):
    mids, (pre, out, pad) = refs[:planes], refs[planes:]
    cells, chans = pre.shape
    col = lax.broadcasted_iota(jnp.int32, (cells, 1), 0) % wid
    rhs = []
    for mid in mids:
        p32 = mid[...].astype(F32)
        left = jnp.where(col < wid - 1, pltpu.roll(p32, cells - 1, 0), 0.0).astype(BF16)
        right = jnp.where(col > 0, pltpu.roll(p32, 1, 0), 0.0).astype(BF16)
        rhs += [left, mid[...], right]
    rhs = jnp.concatenate(rhs, axis=1)
    lane_group = lax.broadcasted_iota(jnp.int32, (group, chans), 1) // group
    zero = jnp.zeros((wid, chans), BF16)
    pad[0:wid, :] = zero
    pad[wid + cells : 2 * wid + cells, :] = zero
    pad[wid : wid + cells, :] = jnp.maximum(pre[...], jnp.zeros((), BF16))
    for t in range(3):
        lhs = pad[t * wid : t * wid + cells, :]
        res = lax.dot_general(lhs, rhs, TN, preferred_element_type=F32)
        for p in range(planes):
            for u in range(3):
                first = (3 * p + u) * chans
                tile = res[:, first : first + chans]
                acc = jnp.zeros((group, chans), F32)
                for g in range(chans // group):
                    acc = jnp.where(lane_group == g, tile[g * group : (g + 1) * group, :], acc)
                out[p, 3 * t + u] = acc.astype(BF16)


def pair_body(here, early, late, other_early, other_late, out):
    odd = here[0] % 2
    out[1] = (early[0].astype(F32) + other_early[0].astype(F32)).astype(BF16)
    out[2 * odd] = (early[1].astype(F32) + other_late[0].astype(F32)).astype(BF16)
    out[2 - 2 * odd] = (late[0].astype(F32) + other_early[1].astype(F32)).astype(BF16)


def total_body(scale, own, other, out):
    for s in range(3):
        out[9 * s : 9 * s + 9] = (own[s].astype(F32) + other[s].astype(F32)) * scale


def back_body(wid, here, mid, near, far, pre, weights, *refs):
    outs, pad = refs[:-1], refs[-1]
    d, h = here[0], here[1]
    cells, chans = mid.shape
    rows = cells // len(outs)
    zero = jnp.zeros((wid, chans), BF16)
    odd = d % 2 == 1
    pad[1, wid : wid + cells, :] = mid[...]
    pad[2, wid : wid + cells, :] = jnp.where(odd, near[...], far[...])
    pad[0, wid : wid + cells, :] = jnp.where(odd, far[...], near[...])
    for s in range(3):
        pad[s, 0:wid, :] = zero
        pad[s, wid + cells : 2 * wid + cells, :] = zero
    col = lax.broadcasted_iota(jnp.int32, (2 * rows, 1), 0) % wid
    chip = h // 2
    for m in range(0, len(outs), 2):
        first = pl.multiple_of(((chip ^ m) // 2) * 2 * rows, wid)
        lhs = jnp.concatenate(
            [pad[s, pl.ds(first + (2 - t) * wid, 2 * rows), :] for s in range(3) for t in range(3)], axis=1
        )
        y = lax.dot_general(lhs, weights[...], NT, preferred_element_type=F32)
        total = y[:, chans : 2 * chans]
        total = total + jnp.where(col < wid - 1, pltpu.roll(y[:, :chans], 2 * rows - 1, 0), 0.0)
        total = total + jnp.where(col > 0, pltpu.roll(y[:, 2 * chans :], 1, 0), 0.0)
        keep = pre[pl.ds(first, 2 * rows), :].astype(F32) > 0
        total = jnp.where(keep, total, 0.0).astype(BF16)
        even = chip % 2 == 0
        outs[m][...] = jnp.where(even, total[:rows], total[rows:])
        outs[m + 1][...] = jnp.where(even, total[rows:], total[:rows])


def partial_body(here, skip, *refs):
    chips = 4
    grads, ws, (own, other, lhs_ref) = refs[:chips], refs[chips:-3], refs[-3:]
    chip, core = here[1] // 2, here[1] % 2
    rows = skip.shape[0]
    for m, grad in enumerate(grads):
        lhs_ref[chip ^ m] = grad[...]
    lhs = jnp.concatenate([lhs_ref[i] for i in range(chips)], axis=1)
    for m, w in enumerate(ws):
        acc = lax.dot_general(lhs, w[...], NT, preferred_element_type=F32)
        width = w.shape[0]
        at = pl.ds(pl.multiple_of((chip ^ m) * width, width), width)
        here_part = jnp.where(core == 0, acc[:rows], acc[rows:])
        there_part = jnp.where(core == 0, acc[rows:], acc[:rows])
        own[:, at] = here_part + skip[:, at].astype(F32)
        other[:, at] = there_part.astype(BF16)


def weights_body(group, kernel, out):
    chans = kernel.shape[2]
    row_group = lax.broadcasted_iota(jnp.int32, (chans, chans), 0) // group
    lane_group = lax.broadcasted_iota(jnp.int32, (chans, chans), 1) // group
    zero = jnp.zeros((chans, chans), BF16)
    for o in range(27):
        st, u = o // 3, o % 3
        tiled = jnp.concatenate([kernel[o]] * (chans // group), axis=0)
        out[u * chans : (u + 1) * chans, st * chans : (st + 1) * chans] = jnp.where(
            row_group == lane_group, tiled, zero
        )


def z_swaps(x):
    n = lax.axis_size("depth")
    between = [(i, i + 1) for i in range(1, n - 1, 2)]
    far = lax.ppermute(x, "depth", between + [(j, i) for i, j in between])
    near = swap(x, "depth", 1)
    return near, far


def fast(grad_out, pre_act, w_in, w_out, kernel):
    _, rows_here, wid, width = grad_out.shape
    _, height, _, chans = pre_act.shape
    group = kernel.shape[1]
    block = rows_here * wid
    cells = height * wid
    d, h = lax.axis_index("depth"), lax.axis_index("height")
    here = jnp.stack([d, h]).astype(jnp.int32)
    skip = grad_out.reshape(block, width)
    pre = pre_act.reshape(cells, chans)

    blocks = chip_gather(skip)
    gathered = plane_gather(blocks)
    part = w_out.shape[0] // 2
    rows = lax.dynamic_slice_in_dim(w_out, h % 2 * part, part, axis=0)
    mine = call(
        pack_body, jax.ShapeDtypeStruct((2, part, width), BF16), 2, nbytes=6 * w_out.size
    )(here, rows, w_in)
    fetched = fetch(mine)
    weights = call(
        functools.partial(weights_body, group),
        jax.ShapeDtypeStruct((3 * chans, 9 * chans), BF16),
        1,
        scalars=0,
        nbytes=54 * chans * chans,
    )(order(kernel, fetched))

    places = [(mask, first) for mask, first, _ in gathered]
    mid = call(
        functools.partial(mid_body, places, block),
        jax.ShapeDtypeStruct((cells, chans), BF16),
        2 + len(places),
        flops=2 * cells * width * chans,
        nbytes=2 * cells * width,
    )(here, mine, fetched, *[b for _, _, b in gathered])

    near, far = z_swaps(mid)
    w_cols = call(
        columns_body, jax.ShapeDtypeStruct((w_in.shape[0], width // 2), BF16), 2, nbytes=2 * w_in.size
    )(here, mine, fetched)
    kernel_flops = 2 * 9 * chans * chans * cells
    early, late = (
        call(
            functools.partial(kgrad_body, wid, group, len(planes)),
            jax.ShapeDtypeStruct((len(planes), 9, group, chans), BF16),
            len(planes) + 1,
            scalars=0,
            scratch=[pltpu.VMEM((cells + 2 * wid, chans), BF16)],
            flops=kernel_flops * len(planes),
            nbytes=6 * cells * chans,
        )(*planes, pre)
        for planes in ((mid, near), (far,))
    )
    w_blocks = [w_cols] + [swap(w_cols, "height", 2 * m) for m in (1, 2)]
    w_blocks.append(swap(w_blocks[1], "height", 4))
    chip_cells = 2 * block
    back = call(
        functools.partial(back_body, wid),
        [jax.ShapeDtypeStruct((chip_cells, chans), BF16)] * (cells // chip_cells),
        5,
        scratch=[pltpu.VMEM((3, cells + 2 * wid, chans), BF16)],
        flops=2 * 27 * chans * chans * cells,
        nbytes=10 * cells * chans,
    )(here, mid, near, far, pre, order(weights, early, late))
    pair = call(
        pair_body,
        jax.ShapeDtypeStruct((3, 9, group, chans), BF16),
        4,
        nbytes=100 * 9 * group * chans,
    )(here, order(early, back[0], w_blocks[1], w_blocks[2]), late, swap(early, "depth", 1), swap(late, "depth", 1))
    total_cells = cells * lax.axis_size("depth")
    other_pair = swap(pair, "depth", 2)
    kernel_grad = call(
        functools.partial(total_body, float(total_cells) ** -0.5),
        jax.ShapeDtypeStruct((27, group, chans), F32),
        2,
        scalars=0,
        flops=SPAN,
        nbytes=24 * 9 * group * chans,
    )(pair, other_pair)

    parts = [back[0]] + [swap(b, "height", 2 * m) for m, b in enumerate(back) if m]

    own, other = call(
        partial_body,
        [jax.ShapeDtypeStruct((block, width), F32), jax.ShapeDtypeStruct((block, width), BF16)],
        1 + len(parts) + len(w_blocks),
        scratch=[pltpu.VMEM((len(parts), chip_cells, chans), BF16)],
        flops=2 * block * width * width,
        nbytes=width * width,
    )(here, order(skip, pair), *parts, *w_blocks)
    theirs = swap(other, "height", 1)
    theirs = order(theirs, kernel_grad)
    grad_in = (own + theirs.astype(F32)).astype(BF16)
    return grad_in.reshape(grad_out.shape), kernel_grad


def with_halo(cells, axis, dim, width):
    head = lax.slice_in_dim(cells, 0, width, axis=dim)
    tail = lax.slice_in_dim(cells, cells.shape[dim] - width, cells.shape[dim], axis=dim)
    return jnp.concatenate([shift(tail, axis, 1), cells, shift(head, axis, -1)], axis=dim)


def general(grad_out, pre_act, w_in, w_out, kernel):
    product = lax.dot_general(
        grad_out,
        lax.all_gather(w_out, "depth", axis=0, tiled=True),
        (((3,), (1,)), ((), ())),
        preferred_element_type=F32,
    )
    grad_mid = product.astype(BF16)
    grouped = lax.all_to_all(grad_mid, "height", split_axis=3, concat_axis=1, tiled=True)
    padded = with_halo(grouped, "depth", 0, 1)
    padded = jnp.pad(padded, ((0, 0), (1, 1), (1, 1), (0, 0)))
    depth_len, height_len, width_len, chans = pre_act.shape
    group = kernel.shape[1]
    groups = chans // group
    hidden = jnp.maximum(pre_act, jnp.zeros_like(pre_act)).reshape(
        depth_len, height_len, width_len, groups, group
    )
    kern = kernel.reshape(27, group, groups, group)
    back = jnp.zeros((groups, group, depth_len, height_len, width_len), F32)
    grads = []
    for s in range(3):
        windows = [
            padded[2 - s : 2 - s + depth_len, 2 - t : 2 - t + height_len, 2 - u : 2 - u + width_len, :]
            for t in range(3)
            for u in range(3)
        ]
        stacked = jnp.concatenate(windows, axis=3)
        stacked = stacked.reshape(depth_len, height_len, width_len, 9, groups, group)
        back = back + jnp.einsum(
            "dhwkgj,kigj->gidhw", stacked, kern[9 * s : 9 * s + 9], preferred_element_type=F32
        )
        grads.append(jnp.einsum("dhwkgj,dhwgi->kigj", stacked, hidden, preferred_element_type=F32))
    back = jnp.transpose(back, (2, 3, 4, 0, 1)).reshape(depth_len, height_len, width_len, chans)
    grad_pre = jnp.where(pre_act > 0, back, jnp.zeros_like(back)).astype(BF16)
    part = jnp.concatenate(grads, axis=0).reshape(27, group, chans)
    total_cells = depth_len * lax.axis_size("depth") * height_len * width_len
    scale = jnp.float32(total_cells) ** (-0.5)
    kernel_grad = lax.psum(part.astype(BF16), "depth").astype(F32) * scale
    by_height = lax.all_to_all(grad_pre, "height", split_axis=1, concat_axis=3, tiled=True)
    branch = lax.dot_general(
        by_height,
        lax.all_gather(w_in, "depth", axis=0, tiled=True),
        (((3,), (1,)), ((), ())),
        preferred_element_type=F32,
    )
    return (grad_out.astype(F32) + branch).astype(BF16), kernel_grad


def solution(mesh):
    planes, cols = mesh.shape["depth"], mesh.shape["height"]

    def shards(grad_out, pre_act, w_in, w_out, kernel):
        whole_lanes = pre_act.shape[3] == 128 and pre_act.shape[0] == 1 and grad_out.shape[0] == 1
        if cols == 8 and planes == 4 and whole_lanes:
            return fast(grad_out, pre_act, w_in, w_out, kernel)
        return general(grad_out, pre_act, w_in, w_out, kernel)

    in_specs = (
        P("depth", "height", None, None),
        P("depth", None, None, "height"),
        P("depth", None),
        P("depth", None),
        P(None, None, "height"),
    )
    out_specs = (P("depth", "height", None, None), P(None, None, "height"))
    return jax.shard_map(shards, mesh=mesh, in_specs=in_specs, out_specs=out_specs, check_vma=False)
```
